128 devices in a mesh: rep: 8 (over x_lo, y), shard: 16 (over x_hi, z, core).
Axes of the slice: x: 4 (x_hi: 2, x_lo: 2; x = x_hi * 2 + x_lo), y: 4, z: 4, core: 2. Of those that a mesh axis runs over, the one named last changes fastest.
Arguments:
- tokens: bfloat16 [32768, 768], P(('rep', 'shard')), may hold values from -6 to 6
- segment_ids: int32 [8, 4096], P('rep'), may hold values from 0 to 15, never falling along the last dimension, each value on 1 to 2000 neighbouring positions
- norm1_gain: bfloat16 [768], P('shard'), may hold values from 0.099609375 to 1.8984375
- w_qkv: bfloat16 [768, 2304], P('shard'), may hold values from -0.21875 to 0.21875
- w_attn_out: bfloat16 [768, 768], P('shard'), may hold values from -1.25 to 1.25
- norm2_gain: bfloat16 [768], P('shard'), may hold values from 0.099609375 to 1.8984375
- w_in: bfloat16 [768, 2304], P('shard'), may hold values from -0.21875 to 0.21875
- w_mlp_out: bfloat16 [1152, 768], P('shard'), may hold values from -0.1875 to 0.1875
- cotangent: bfloat16 [32768, 768], P(('rep', 'shard')), may hold values from -24 to 24
Outputs:
- output: bfloat16 [32768, 768], P(('rep', 'shard'))
- grad_tokens: bfloat16 [32768, 768], P(('rep', 'shard'))
- grad_norm1_gain: float32 [768], P('shard')
- grad_w_qkv: float32 [768, 2304], P('shard')
- grad_w_attn_out: float32 [768, 768], P('shard')
- grad_norm2_gain: float32 [768], P('shard')
- grad_w_in: float32 [768, 2304], P('shard')
- grad_w_mlp_out: float32 [1152, 768], P('shard')
The draws below stay inside these ranges and needn't reach their ends.
Inputs may be any that keep to these rules, and one draw needn't show every extreme that they name: `segment_ids`: along a sequence the ids never fall; each id from 0 to 15 is used by 1 to 2000 consecutive tokens, and one document has exactly 2000.
All inputs are finite; a program needn't handle non-finite values.
Results may differ from the reference program's by a relative error of at most 0.025.
Values may be sent and summed in bfloat16 or wider, within the bound.
No kernel may reach another device: no remote copies, remote signals or barrier semaphores. Data moves between devices by JAX's collectives and lax.ppermute only.
A program may use at most 128 MiB of HBM per device.

```python
import math
import jax
import jax.numpy as jnp
import numpy as np
from jax import lax

D = 768
HEADS = 12
HEAD = 64
FF = 1152
HALF = 64
SEQ = 4096
SEQS = 8
TOKENS = 32768
DOCS = 16
DOC_MOST = 2000


def strengthened(values, own_key, source, target, blocks, factor):
    owner, partner = [(jnp.arange(values.shape[axis_at]) // (values.shape[axis_at] // blocks)).reshape([-1 if axis == axis_at else 1 for axis in range(values.ndim)]) for axis_at in (source, target)]
    chosen = jax.random.permutation(own_key, blocks)[partner]
    strong = (owner == chosen) | (owner == (partner + blocks // 2) % blocks)
    return jnp.where(strong, factor * values, values)


def shard_levels(stream_key, extent, split, smallest, top_value):
    def one(dim, shards_of):
        steps = jax.random.uniform(jax.random.fold_in(jax.random.fold_in(stream_key, 6), dim), (shards_of,), jnp.float32, smallest / len(split), top_value / len(split))
        return jnp.repeat(jnp.exp(steps), extent[dim] // shards_of).reshape((-1,) + (1,) * (len(extent) - dim - 1))

    loudness = one(*split[0])
    for cut in split[1:]:
        loudness = loudness * one(*cut)
    return loudness


def profile(count, total, limit, skew):
    loads = [(1 << 20) // math.isqrt(standing ** skew) + 1 for standing in range(2, count + 1)]
    spare, given = total - limit - (count - 1), [1] * (count - 1)
    while spare > 0:
        free = [i for i in range(count - 1) if given[i] < limit]
        whole, left = sum([loads[i] for i in free]), spare
        for i in free:
            addition = min(limit - given[i], max(1, left * loads[i] // whole), spare)
            given[i] = given[i] + addition
            spare = spare - addition
    return np.array([limit] + given)


def uneven_parts(stream_key, amount, total, reach, slope):
    if amount == 2:
        one = jax.random.randint(stream_key, (), max(1, total - reach), min(reach, total - 1) + 1)
        return jnp.stack([one, total - one])
    lengths = jnp.asarray(profile(amount, total, reach, slope), jnp.int32)
    pairs = (amount - 1) // 2
    giver, receiver = lengths[1:1 + 2 * pairs:2], lengths[2:2 + 2 * pairs:2]
    slack = jnp.minimum(giver - 1, reach - receiver)
    shifted = jax.random.randint(jax.random.fold_in(stream_key, 1), (pairs,), 0, 1 << 20) % (slack + 1)
    lengths = lengths.at[1:1 + 2 * pairs:2].set(giver - shifted).at[2:2 + 2 * pairs:2].set(receiver + shifted)
    return lengths[jax.random.permutation(jax.random.fold_in(stream_key, 2), amount)]


def gaussian(stream_key, extent, width, reach, shards=(), kind=jnp.bfloat16):
    array = width * jax.random.normal(stream_key, extent, jnp.float32)
    if shards:
        array = array * shard_levels(stream_key, extent, shards, -0.22, 0.18)
    return jnp.clip(array, -reach, reach).astype(kind)


def bell_draw_with(rng, dims, deviation, most, split, heavy, held_as=jnp.bfloat16):
    values = deviation * jax.random.normal(rng, dims, jnp.float32)
    if split:
        values = values * shard_levels(rng, dims, split, -0.22, 0.18)
    return jnp.clip(strengthened(values, jax.random.fold_in(rng, 3), *heavy), -most, most).astype(held_as)


def setup_inputs(seed: int = 0) -> dict:
    arg_keys = jax.random.split(jax.random.key(seed), 10)
    tokens = gaussian(arg_keys[0], (TOKENS, D), 1.0, 6.0, ((0, 128),))
    segment_ids = jax.vmap(lambda own: jnp.searchsorted(jnp.cumsum(uneven_parts(own, DOCS, SEQ, DOC_MOST, 1)), jnp.arange(SEQ), side="right"))(jax.random.split(arg_keys[1], SEQS)).reshape((SEQS, SEQ)).astype(jnp.int32)
    norm1_gain = jnp.clip(1.0 + 0.18 * jax.random.normal(arg_keys[2], (D,), jnp.float32), 0.099609375, 1.8984375).astype(jnp.bfloat16)
    w_qkv = gaussian(arg_keys[3], (D, 3 * D), D ** -0.5, 0.21875, ((0, 16),))
    w_attn_out = gaussian(arg_keys[4], (D, D), (D // 32) ** -0.5, 1.25, ((0, 16),))
    norm2_gain = jnp.clip(1.0 + 0.18 * jax.random.normal(arg_keys[5], (D,), jnp.float32), 0.099609375, 1.8984375).astype(jnp.bfloat16)
    w_in = gaussian(arg_keys[6], (D, 2 * FF), D ** -0.5, 0.21875, ((0, 16),))
    w_mlp_out = gaussian(arg_keys[7], (FF, D), FF ** -0.5, 0.1875, ((0, 16),))
    cotangent = bell_draw_with(arg_keys[8], (TOKENS, D), 1.0, 24.0, ((0, 128),), (0, 1, 128, 5.5))
    return dict(tokens=tokens, segment_ids=segment_ids, norm1_gain=norm1_gain, w_qkv=w_qkv, w_attn_out=w_attn_out, norm2_gain=norm2_gain, w_in=w_in, w_mlp_out=w_mlp_out, cotangent=cotangent)


@jax.custom_vjp
def reduced_precision(v):
    return lax.optimization_barrier(v.astype(jnp.bfloat16)).astype(jnp.float32)

@jax.custom_vjp
def low_back(v):
    return v

def low_keep(v):
    return (reduced_precision(v), None)

def low_pass(kept, grad):
    return (grad,)

def back_keep(v):
    return (v, None)

def back_low(kept, grad):
    return (reduced_precision(grad),)
reduced_precision.defvjp(low_keep, low_pass)
low_back.defvjp(back_keep, back_low)
precise = lax.Precision.HIGHEST
norm_epsilon = 1e-05
masked_score = -1e+30

def apply_layer_norm(values):
    centre = values - lax.optimization_barrier(jnp.mean(values, axis=-1, keepdims=True))
    spread = lax.optimization_barrier(jnp.mean(centre * centre, axis=-1, keepdims=True))
    return centre * lax.rsqrt(spread + norm_epsilon)

def rotate(vectors, cosine_table, sine_table):
    half_size = vectors.shape[-1] // 2
    turned = jnp.concatenate([-vectors[..., half_size:], vectors[..., :half_size]], axis=-1)
    return vectors * cosine_table + turned * sine_table

def angles(position, head_width):
    fractions = jnp.arange(0, head_width, 2).astype(jnp.float32) / head_width
    inverse = jnp.exp(-math.log(10000.0) * fractions)
    phases = position.astype(jnp.float32)[:, None] * inverse[None, :]
    phases = jnp.concatenate([phases, phases], axis=-1)
    return (jnp.cos(phases)[:, None, :], jnp.sin(phases)[:, None, :])

def doc_positions(seq_segs):
    seq_length = seq_segs.shape[0]
    doc_index = jnp.arange(DOCS, dtype=jnp.int32)
    starts = lax.optimization_barrier(jnp.sum((seq_segs[None, :] < doc_index[:, None]).astype(jnp.int32), axis=1))
    onehot = (seq_segs[:, None] == doc_index[None, :]).astype(jnp.int32)
    return jnp.arange(seq_length, dtype=jnp.int32) - lax.optimization_barrier(jnp.sum(onehot * starts[None, :], axis=1))

def attend(queries, key_all, value_all, seq_segs):
    query_block = min(512, SEQ)
    blocks = SEQ // query_block
    key_span = query_block + 2 * HALF
    keys_pad = jnp.pad(key_all, ((HALF, HALF), (0, 0), (0, 0)))
    values_pad = jnp.pad(value_all, ((HALF, HALF), (0, 0), (0, 0)))
    segs_pad = jnp.pad(seq_segs, (HALF, HALF), constant_values=-1)
    row_index = jnp.arange(query_block, dtype=jnp.int32)[:, None] + HALF
    column_index = jnp.arange(key_span, dtype=jnp.int32)[None, :]
    within_reach = jnp.abs(row_index - column_index) <= HALF
    score_scale = 1.0 / math.sqrt(HEAD)

    def one_block(begin):
        query_rows = lax.dynamic_slice_in_dim(queries, begin, query_block, 0)
        key_rows = lax.dynamic_slice_in_dim(keys_pad, begin, key_span, 0)
        value_rows = lax.dynamic_slice_in_dim(values_pad, begin, key_span, 0)
        query_segs = lax.dynamic_slice_in_dim(segs_pad, begin + HALF, query_block, 0)
        key_segs = lax.dynamic_slice_in_dim(segs_pad, begin, key_span, 0)
        allowed = within_reach & (query_segs[:, None] == key_segs[None, :])
        raw_scores = jnp.einsum('qhd,khd->hqk', query_rows, key_rows, precision=precise)
        scores = low_back(raw_scores * score_scale)
        scores = jnp.where(allowed[None], scores, masked_score)
        row_max = lax.optimization_barrier(jnp.max(scores, axis=-1, keepdims=True))
        exponent = jnp.exp(scores - row_max)
        attn_probs = exponent / lax.optimization_barrier(jnp.sum(exponent, axis=-1, keepdims=True))
        return jnp.einsum('hqk,khd->qhd', reduced_precision(attn_probs), value_rows, precision=precise)
    starts = jnp.arange(blocks, dtype=jnp.int32) * query_block
    blocks_out = lax.map(jax.checkpoint(one_block), starts)
    return blocks_out.reshape(SEQ, HEADS * HEAD)

def layer(sequence_rows, single_gain_vector, weight_qkv, weight_out, gain_two, weight_in, weight_down, cosine_table, sine_table, seq_segs):
    first_standardized = apply_layer_norm(sequence_rows)
    first_normalized = reduced_precision(first_standardized * single_gain_vector)
    qkv_all = low_back(jnp.dot(first_normalized, weight_qkv, precision=precise, preferred_element_type=jnp.float32))
    split_parts = qkv_all.reshape(SEQ, 3, HEADS, HEAD)
    queries = reduced_precision(rotate(split_parts[:, 0], cosine_table, sine_table))
    key_all = reduced_precision(rotate(split_parts[:, 1], cosine_table, sine_table))
    value_all = reduced_precision(split_parts[:, 2])
    context = reduced_precision(low_back(attend(queries, key_all, value_all, seq_segs)))
    attn_out = low_back(jnp.dot(context, weight_out, precision=precise, preferred_element_type=jnp.float32))
    hidden_rows = sequence_rows + attn_out
    second_normalized = reduced_precision(apply_layer_norm(hidden_rows) * gain_two)
    gate_up = low_back(jnp.dot(second_normalized, weight_in, precision=precise, preferred_element_type=jnp.float32))
    mixed_rows = reduced_precision(jax.nn.gelu(gate_up[:, :FF], approximate=False) * gate_up[:, FF:])
    mlp_out = low_back(jnp.dot(mixed_rows, weight_down, precision=precise, preferred_element_type=jnp.float32))
    return hidden_rows + mlp_out

def reference(tokens, segment_ids, norm1_gain, w_qkv, w_attn_out, norm2_gain, w_in, w_mlp_out, cotangent):
    weights = (norm1_gain.astype(jnp.float32), w_qkv.astype(jnp.float32), w_attn_out.astype(jnp.float32), norm2_gain.astype(jnp.float32), w_in.astype(jnp.float32), w_mlp_out.astype(jnp.float32))
    input_rows = tokens.astype(jnp.float32).reshape(SEQS, SEQ, D)
    cotangent_seq = cotangent.astype(jnp.float32).reshape(SEQS, SEQ, D)

    def per_sequence(totals, sequence_item):
        sequence_rows, seq_segs, grad_out = sequence_item
        cosine_table, sine_table = angles(doc_positions(seq_segs), HEAD)

        def forward(rows_in, single_gain_vector, weight_qkv, weight_out, gain_two, weight_in, weight_down):
            return layer(rows_in, single_gain_vector, weight_qkv, weight_out, gain_two, weight_in, weight_down, cosine_table, sine_table, seq_segs)
        result, pullback = jax.vjp(forward, sequence_rows, weights[0], weights[1], weights[2], weights[3], weights[4], weights[5])
        gradients = pullback(grad_out)
        totals = tuple((total + gradient for total, gradient in zip(totals, gradients[1:])))
        return (totals, (result.astype(jnp.bfloat16), gradients[0].astype(jnp.bfloat16)))
    zero_grads = tuple((jnp.zeros(weight.shape, jnp.float32) for weight in weights))
    totals, (outputs, grad_inputs) = lax.scan(per_sequence, zero_grads, (input_rows, segment_ids, cotangent_seq))
    return (outputs.reshape(TOKENS, D), grad_inputs.reshape(TOKENS, D), totals[0], totals[1], totals[2], totals[3], totals[4], totals[5])
```

```python
import math

import jax
import jax.numpy as jnp
from jax import lax
from jax.experimental import pallas as pl
from jax.experimental.pallas import tpu as pltpu
from jax.sharding import PartitionSpec as P

HEADS = 12
HEAD = 64
HALF = 64
WIDTH = 768
AXES = ("rep", "shard")
BF = jnp.bfloat16
F32 = jnp.float32

norm_epsilon = 1e-05
masked_score = -1e30
root_half = 0.7071067811865476
density_factor = 0.3989422804014327


def coordinates(device):
    rep, shard = divmod(device, 16)
    x_low, y = divmod(rep, 4)
    x_high, rest = divmod(shard, 8)
    z, core = divmod(rest, 2)
    return x_high * 2 + x_low, y, z, core


def number(x, y, z, core):
    return ((x % 2) * 4 + y) * 16 + (x // 2) * 8 + z * 2 + core


def pairs(move):
    return [(device, number(*move(*coordinates(device)))) for device in range(128)]


def along_z(step):
    return pairs(lambda x, y, z, core: (x, y, (z + step) % 4, core))


def along_y(step):
    return pairs(lambda x, y, z, core: (x, (y + step) % 4, z, core))


OTHER_CORE = pairs(lambda x, y, z, core: (x, y, z, 1 - core))
ACROSS_X = pairs(lambda x, y, z, core: (3 - x, y, z, core))
TWIN_X = pairs(lambda x, y, z, core: (x ^ 1, y, z, core))
Z_STEP = {step: along_z(step) for step in (1, 2, 3)}
Y_STEP = {step: along_y(step) for step in (1, 2, 3)}


def send(value, route):
    return lax.ppermute(value, AXES, route)


def place():
    shard = lax.axis_index("shard")
    rep = lax.axis_index("rep")
    return {
        "x_high": shard // 8,
        "z": (shard // 2) % 4,
        "core": shard % 2,
        "x_low": rep // 4,
        "y": rep % 4,
        "shard": shard,
    }


PIECES = [(0, 0), (1, 0), (0, 3), (0, 1), (0, 2), (1, 3), (1, 1), (1, 2)]


def gather_group(piece):
    own = {(0, 0): piece}
    own[1, 0] = send(piece, ACROSS_X)
    own[0, 3] = send(piece, Z_STEP[1])
    own[0, 1] = send(piece, Z_STEP[3])
    own[0, 2] = send(piece, Z_STEP[2])
    own[1, 3] = send(own[1, 0], Z_STEP[1])
    own[1, 1] = send(own[1, 0], Z_STEP[3])
    own[1, 2] = send(own[0, 2], ACROSS_X)
    mine = [own[key] for key in PIECES]
    return mine + [send(value, OTHER_CORE) for value in mine]


def row_blocks(where_ref):
    x_high, z, core = where_ref[0], where_ref[1], where_ref[2]
    blocks = []
    for turned, step in PIECES:
        side = 1 - x_high if turned else x_high
        blocks.append((side * 4 + lax.rem(z + step, 4)) * 2)
    return [b + core for b in blocks] + [b + 1 - core for b in blocks]


def at_rows(block, count):
    return pl.ds(pl.multiple_of(block * count, 16), count)


def assemble_first(where_ref, *refs):
    pieces, (weight_ref, gain_ref) = refs[:16], refs[16:]
    total = jnp.zeros((16, WIDTH), F32)
    for block, piece in zip(row_blocks(where_ref), pieces):
        for part in range(3):
            weight_ref[at_rows(block, 48), part * WIDTH : (part + 1) * WIDTH] = piece[
                part * 48 : (part + 1) * 48, :
            ]
        total = total + piece[144:160, :].astype(F32)
    gain_ref[...] = total


def assemble_second(where_ref, *refs):
    pieces, (out_ref, in_ref, down_ref) = refs[:16], refs[16:]
    blocks = row_blocks(where_ref)
    for block, piece in zip(blocks, pieces):
        out_ref[at_rows(block, 48), :] = piece[0:48, :]
        for part in range(3):
            in_ref[at_rows(block, 48), part * WIDTH : (part + 1) * WIDTH] = piece[
                (part + 1) * 48 : (part + 2) * 48, :
            ]
    core = where_ref[2]
    for mine, other, block in zip(pieces[:8], pieces[8:], blocks[:8]):
        here = mine[192:272, :].astype(F32)[:72]
        there = other[192:272, :].astype(F32)[:72]
        first = jnp.where(core == 0, here, there)
        second = jnp.where(core == 0, there, here)
        down_ref[at_rows(block // 2, 144), :] = jnp.concatenate([first, second], axis=0).astype(BF)


def whole_in_vmem(count):
    return [pl.BlockSpec(memory_space=pltpu.VMEM) for _ in range(count)]


def call(kernel, where, arrays, outs):
    return pl.pallas_call(
        kernel,
        out_shape=[jax.ShapeDtypeStruct(shape, kind) for shape, kind in outs],
        in_specs=[pl.BlockSpec(memory_space=pltpu.SMEM)] + whole_in_vmem(len(arrays)),
        out_specs=whole_in_vmem(len(outs)),
        compiler_params=pltpu.CompilerParams(vmem_limit_bytes=48 * 1024 * 1024),
    )(where, *arrays)


def take(values, index, axis):
    return lax.dynamic_index_in_dim(values, index, axis=axis, keepdims=False)


def core_sum(term, at, rows):
    split = term.reshape(8, 2, rows, WIDTH)
    arrived = send(take(split, 1 - at["core"], 1), OTHER_CORE)
    mine = take(split, at["core"], 1)
    return (mine.astype(F32) + arrived.astype(F32)).astype(BF).reshape(2, 4, rows, WIDTH)


def z_sum(blocks, at, axis):
    arrived = [send(take(blocks, (at["z"] + step) % 4, axis), Z_STEP[step]) for step in (1, 3, 2)]
    total = take(blocks, at["z"], axis).astype(F32)
    for value in arrived:
        total = total + value.astype(F32)
    return total.astype(BF)


def x_sum(blocks, at):
    arrived = send(take(blocks, 1 - at["x_high"], 0), ACROSS_X)
    return (take(blocks, at["x_high"], 0).astype(F32) + arrived.astype(F32)).astype(BF)


def shard_sum(blocks, at, cut):
    z_first = x_sum(z_sum(blocks[:, :, :cut], at, 1), at)
    x_first = z_sum(x_sum(blocks[:, :, cut:], at), at, 0)
    return jnp.concatenate([z_first, x_first], axis=0)


def rep_sum(block, at):
    rows = block.shape[0] // 4
    parts = block.reshape(4, rows, WIDTH)
    arrived = [send(take(parts, (at["y"] + step) % 4, 0), Y_STEP[step]) for step in (1, 3, 2)]
    total = take(parts, at["y"], 0).astype(F32)
    for value in arrived:
        total = total + value.astype(F32)
    total = total.astype(BF)
    total = (total.astype(F32) + send(total, TWIN_X).astype(F32)).astype(BF)
    ring = [total] + [send(total, Y_STEP[4 - step]) for step in (1, 2, 3)]
    ring = jnp.stack(ring + ring[:3])
    ordered = lax.dynamic_slice_in_dim(ring, (4 - at["y"]) % 4, 4, axis=0)
    return ordered.reshape(4 * rows, WIDTH)


def normalize_rows(values):
    centre = values - jnp.mean(values, axis=-1, keepdims=True)
    spread = jnp.mean(centre * centre, axis=-1, keepdims=True)
    row_inverse_scale = lax.rsqrt(spread + norm_epsilon)
    return (centre * row_inverse_scale, row_inverse_scale)


def norm_backward_pass(normalized_gradient, standardized_rows, row_inverse_scale):
    centered_average = jnp.mean(normalized_gradient, axis=-1, keepdims=True)
    projected_average = jnp.mean(normalized_gradient * standardized_rows, axis=-1, keepdims=True)
    return row_inverse_scale * (
        normalized_gradient - centered_average - standardized_rows * projected_average
    )


def rotate(vectors, cosine_table, sine_table):
    half_size = vectors.shape[-1] // 2
    turned = jnp.concatenate([-vectors[..., half_size:], vectors[..., :half_size]], axis=-1)
    return vectors * cosine_table + turned * sine_table


def rotate_back(vectors, cosine_table, sine_table):
    half_size = vectors.shape[-1] // 2
    scaled = vectors * sine_table
    turned = jnp.concatenate([scaled[..., half_size:], -scaled[..., :half_size]], axis=-1)
    return vectors * cosine_table + turned


def angles(position, head_width):
    fractions = jnp.arange(0, head_width, 2).astype(jnp.float32) / head_width
    inverse = jnp.exp(-math.log(10000.0) * fractions)
    phases = position.astype(jnp.float32)[:, None] * inverse[None, :]
    phases = jnp.concatenate([phases, phases], axis=-1)
    return (jnp.cos(phases)[:, None, :], jnp.sin(phases)[:, None, :])


def neighbours(count, step):
    return [(i, i + step) for i in range(count) if 0 <= i + step < count]


def by_shard(term):
    return term.astype(BF).reshape(16, term.shape[0] // 16, term.shape[1])


def gain_rows(gain):
    row = jnp.zeros((8, WIDTH), F32).at[0].set(gain).astype(BF)
    return jnp.broadcast_to(row[None], (16, 8, WIDTH))


def shards(
    tokens, segment_ids, norm1_gain, w_qkv, w_attn_out, norm2_gain, w_in, w_mlp_out, cotangent
):
    row_count = tokens.shape[0]
    model_width = tokens.shape[1]
    hidden_units = w_in.shape[1] // 2
    head_count = HEADS
    head_size = HEAD
    rim_width = HALF
    key_span = row_count + 2 * rim_width
    score_scale = 1.0 / math.sqrt(head_size)
    at = place()
    where = jnp.stack([at["x_high"], at["z"], at["core"]]).astype(jnp.int32)
    shard_place = at["shard"]

    gains = jnp.stack([norm1_gain, norm2_gain])
    spread_gains = lax.dynamic_update_slice(
        jnp.zeros((16, WIDTH), BF), gains, (jnp.zeros((), jnp.int32), shard_place * 48)
    )
    first_piece = jnp.concatenate(
        [w_qkv[:, :WIDTH], w_qkv[:, WIDTH : 2 * WIDTH], w_qkv[:, 2 * WIDTH :], spread_gains]
    )
    second_piece = jnp.concatenate(
        [
            w_attn_out,
            w_in[:, :WIDTH],
            w_in[:, WIDTH : 2 * WIDTH],
            w_in[:, 2 * WIDTH :],
            w_mlp_out,
            jnp.zeros((8, WIDTH), BF),
        ]
    )
    wqkv_all, gain_table = call(
        assemble_first,
        where,
        gather_group(first_piece),
        [((WIDTH, 3 * WIDTH), BF), ((16, WIDTH), F32)],
    )
    first_norm_gains, second_norm_gains = gain_table[0], gain_table[1]
    wout_all, win_all, wdown_all = call(
        assemble_second,
        where,
        gather_group(second_piece),
        [((WIDTH, WIDTH), BF), ((WIDTH, 3 * WIDTH), BF), ((1152, WIDTH), BF)],
    )

    first_row = shard_place * row_count
    seq_segs = segment_ids[0]
    own_segs = lax.dynamic_slice_in_dim(seq_segs, first_row, row_count, 0)
    earlier = jnp.sum((seq_segs[None, :] < own_segs[:, None]).astype(jnp.int32), axis=1)
    position = jnp.arange(row_count, dtype=jnp.int32) + first_row - earlier
    cosine_table, sine_table = angles(position, head_size)
    segs_pad = jnp.pad(seq_segs, (rim_width, rim_width), constant_values=-1)
    key_segs = lax.dynamic_slice_in_dim(segs_pad, first_row, key_span, 0)
    row_index = jnp.arange(row_count, dtype=jnp.int32)[:, None] + rim_width
    column_index = jnp.arange(key_span, dtype=jnp.int32)[None, :]
    allowed = (jnp.abs(row_index - column_index) <= rim_width) & (
        own_segs[:, None] == key_segs[None, :]
    )
    input_rows = tokens.astype(jnp.float32)
    first_standardized, first_inverse_scale = normalize_rows(input_rows)
    first_normalized = (first_standardized * first_norm_gains).astype(jnp.bfloat16)
    qkv_all = jnp.dot(first_normalized, wqkv_all, preferred_element_type=jnp.float32)
    split_parts = qkv_all.reshape(row_count, 3, head_count, head_size)
    queries = rotate(split_parts[:, 0], cosine_table, sine_table).astype(jnp.bfloat16)
    key_rows = rotate(split_parts[:, 1], cosine_table, sine_table).astype(jnp.bfloat16)
    values = split_parts[:, 2].astype(jnp.bfloat16)
    joined = jnp.concatenate(
        [key_rows.reshape(row_count, model_width), values.reshape(row_count, model_width)], axis=1
    )
    joined_ext = jnp.concatenate(
        [
            lax.ppermute(joined[row_count - rim_width :], "shard", neighbours(16, 1)),
            joined,
            lax.ppermute(joined[:rim_width], "shard", neighbours(16, -1)),
        ]
    )
    keys_ext = joined_ext[:, :model_width].reshape(key_span, head_count, head_size)
    values_ext = joined_ext[:, model_width:].reshape(key_span, head_count, head_size)

    def scores_of():
        raw_scores = (
            jnp.einsum("qhd,khd->hqk", queries, keys_ext, preferred_element_type=jnp.float32)
            * score_scale
        )
        return jnp.where(allowed[None], raw_scores, masked_score)

    scores = scores_of()
    row_max = jnp.max(scores, axis=-1, keepdims=True)
    exponent = jnp.exp(scores - row_max)
    row_total = jnp.sum(exponent, axis=-1, keepdims=True)
    log_total = row_max + jnp.log(row_total)
    probs_low = (exponent / row_total).astype(jnp.bfloat16)
    context = jnp.einsum("hqk,khd->qhd", probs_low, values_ext, preferred_element_type=jnp.float32)
    context = context.reshape(row_count, model_width).astype(jnp.bfloat16)
    attn_out = jnp.dot(context, wout_all, preferred_element_type=jnp.float32)
    hidden_rows = input_rows + attn_out
    second_standardized, second_inverse_scale = normalize_rows(hidden_rows)
    second_normalized = (second_standardized * second_norm_gains).astype(jnp.bfloat16)
    gate_up = jnp.dot(second_normalized, win_all, preferred_element_type=jnp.float32)
    gate_part = gate_up[:, :hidden_units]
    up_part = gate_up[:, hidden_units:]
    activated = jax.nn.gelu(gate_part, approximate=False)
    mixed_rows = (activated * up_part).astype(jnp.bfloat16)
    mlp_out = jnp.dot(mixed_rows, wdown_all, preferred_element_type=jnp.float32)
    output = (hidden_rows + mlp_out).astype(jnp.bfloat16)
    grad_out = cotangent.astype(jnp.float32)
    term_down = jnp.einsum("tf,td->fd", mixed_rows, cotangent, preferred_element_type=jnp.float32)
    grad_mixed = jnp.einsum("td,fd->tf", cotangent, wdown_all, preferred_element_type=jnp.float32)
    normal_cdf = 0.5 * (1.0 + lax.erf(gate_part * root_half))
    normal_pdf = jnp.exp(-0.5 * gate_part * gate_part) * density_factor
    grad_gate = grad_mixed * up_part * (normal_cdf + gate_part * normal_pdf)
    grad_up = grad_mixed * activated
    grad_gate_up = jnp.concatenate([grad_gate, grad_up], axis=1).astype(jnp.bfloat16)
    term_in = [
        jnp.einsum(
            "td,tf->df",
            second_normalized,
            grad_gate_up[:, part * WIDTH : (part + 1) * WIDTH],
            preferred_element_type=jnp.float32,
        )
        for part in range(3)
    ]
    second_normalized_gradient = jnp.einsum(
        "tf,df->td", grad_gate_up, win_all, preferred_element_type=jnp.float32
    )
    second_gain_term = jnp.sum(second_normalized_gradient * second_standardized, axis=0)
    hidden_gradient = grad_out + norm_backward_pass(
        second_normalized_gradient * second_norm_gains,
        second_standardized,
        second_inverse_scale,
    )
    mlp_terms = jnp.concatenate(
        [by_shard(term) for term in term_in] + [by_shard(term_down), gain_rows(second_gain_term)],
        axis=1,
    )
    mlp_block = shard_sum(core_sum(mlp_terms, at, 224), at, 112)

    grad_attn = hidden_gradient.astype(jnp.bfloat16)
    term_out = jnp.einsum("td,te->de", context, grad_attn, preferred_element_type=jnp.float32)
    grad_context = jnp.einsum("te,de->td", grad_attn, wout_all, preferred_element_type=jnp.float32)
    grad_context = grad_context.astype(jnp.bfloat16).reshape(row_count, head_count, head_size)
    attn_probs = jnp.exp(scores_of() - log_total)
    probs_again = attn_probs.astype(jnp.bfloat16)
    grad_probs = jnp.einsum(
        "qhd,khd->hqk", grad_context, values_ext, preferred_element_type=jnp.float32
    )
    inner = jnp.sum(attn_probs * grad_probs, axis=-1, keepdims=True)
    grad_scores = (attn_probs * (grad_probs - inner)).astype(jnp.bfloat16)
    grad_queries = (
        jnp.einsum("hqk,khd->qhd", grad_scores, keys_ext, preferred_element_type=jnp.float32)
        * score_scale
    )
    grad_keys_ext = (
        jnp.einsum("hqk,qhd->khd", grad_scores, queries, preferred_element_type=jnp.float32)
        * score_scale
    )
    grad_values_ext = jnp.einsum(
        "hqk,qhd->khd", probs_again, grad_context, preferred_element_type=jnp.float32
    )
    grad_joined = jnp.concatenate(
        [
            grad_keys_ext.reshape(key_span, model_width),
            grad_values_ext.reshape(key_span, model_width),
        ],
        axis=1,
    )
    from_below = lax.ppermute(
        grad_joined[row_count + rim_width :].astype(jnp.bfloat16), "shard", neighbours(16, 1)
    ).astype(jnp.float32)
    from_above = lax.ppermute(
        grad_joined[:rim_width].astype(jnp.bfloat16), "shard", neighbours(16, -1)
    ).astype(jnp.float32)
    own_grads = grad_joined[rim_width : rim_width + row_count]
    own_grads = jnp.concatenate(
        [
            own_grads[:rim_width] + from_below,
            own_grads[rim_width : row_count - rim_width],
            own_grads[row_count - rim_width :] + from_above,
        ]
    )
    grad_keys = own_grads[:, :model_width].reshape(row_count, head_count, head_size)
    grad_values = own_grads[:, model_width:]
    grad_qkv = jnp.concatenate(
        [
            rotate_back(grad_queries, cosine_table, sine_table).reshape(row_count, model_width),
            rotate_back(grad_keys, cosine_table, sine_table).reshape(row_count, model_width),
            grad_values,
        ],
        axis=1,
    ).astype(jnp.bfloat16)
    term_qkv = [
        jnp.einsum(
            "td,te->de",
            first_normalized,
            grad_qkv[:, part * WIDTH : (part + 1) * WIDTH],
            preferred_element_type=jnp.float32,
        )
        for part in range(3)
    ]
    first_normalized_gradient = jnp.einsum(
        "te,de->td", grad_qkv, wqkv_all, preferred_element_type=jnp.float32
    )
    first_gain_term = jnp.sum(first_normalized_gradient * first_standardized, axis=0)
    grad_tokens = (
        hidden_gradient
        + norm_backward_pass(
            first_normalized_gradient * first_norm_gains,
            first_standardized,
            first_inverse_scale,
        )
    ).astype(jnp.bfloat16)
    attn_terms = jnp.concatenate(
        [by_shard(term) for term in term_qkv] + [by_shard(term_out), gain_rows(first_gain_term)],
        axis=1,
    )
    attn_block = shard_sum(core_sum(attn_terms, at, 200), at, 96)
    total = rep_sum(jnp.concatenate([mlp_block, attn_block]), at).astype(F32)

    def own_gain(row):
        return lax.dynamic_slice_in_dim(row, shard_place * 48, 48)

    attn_total = total[224:]
    return (
        output,
        grad_tokens,
        own_gain(attn_total[192]),
        jnp.concatenate([attn_total[0:48], attn_total[48:96], attn_total[96:144]], axis=1),
        attn_total[144:192],
        own_gain(total[216]),
        jnp.concatenate([total[0:48], total[48:96], total[96:144]], axis=1),
        total[144:216],
    )


def solution(mesh):
    return jax.shard_map(
        shards,
        mesh=mesh,
        in_specs=(
            P(("rep", "shard"), None),
            P("rep", None),
            P("shard"),
            P("shard", None),
            P("shard", None),
            P("shard"),
            P("shard", None),
            P("shard", None),
            P(("rep", "shard"), None),
        ),
        out_specs=(
            P(("rep", "shard"), None),
            P(("rep", "shard"), None),
            P("shard"),
            P("shard", None),
            P("shard", None),
            P("shard"),
            P("shard", None),
            P("shard", None),
        ),
        check_vma=False,
    )
```

```python
import functools
import math

import jax
import jax.numpy as jnp
from jax import lax
from jax.experimental import pallas as pl
from jax.experimental.pallas import tpu as pltpu
from jax.sharding import PartitionSpec as P

HEADS = 12
HEAD = 64
HALF = 64
WIDTH = 768
AXES = ("rep", "shard")
BF = jnp.bfloat16
F32 = jnp.float32

norm_epsilon = 1e-05
masked_score = -1e30
root_half = 0.7071067811865476
density_factor = 0.3989422804014327
score_scale = 0.125


def coordinates(device):
    rep, shard = divmod(device, 16)
    x_low, y = divmod(rep, 4)
    x_high, rest = divmod(shard, 8)
    z, core = divmod(rest, 2)
    return x_high * 2 + x_low, y, z, core


def number(x, y, z, core):
    return ((x % 2) * 4 + y) * 16 + (x // 2) * 8 + z * 2 + core


def pairs(move):
    return [(device, number(*move(*coordinates(device)))) for device in range(128)]


def along_z(step):
    return pairs(lambda x, y, z, core: (x, y, (z + step) % 4, core))


def along_y(step):
    return pairs(lambda x, y, z, core: (x, (y + step) % 4, z, core))


OTHER_CORE = pairs(lambda x, y, z, core: (x, y, z, 1 - core))
ACROSS_X = pairs(lambda x, y, z, core: (3 - x, y, z, core))
TWIN_X = pairs(lambda x, y, z, core: (x ^ 1, y, z, core))
Z_STEP = {step: along_z(step) for step in (1, 2, 3)}
Y_STEP = {step: along_y(step) for step in (1, 2, 3)}


def send(value, route):
    return lax.ppermute(value, AXES, route)


def place():
    shard = lax.axis_index("shard")
    rep = lax.axis_index("rep")
    return {
        "x_high": shard // 8,
        "z": (shard // 2) % 4,
        "core": shard % 2,
        "x_low": rep // 4,
        "y": rep % 4,
        "shard": shard,
    }


PIECES = [(0, 0), (1, 0), (0, 3), (0, 1), (0, 2), (1, 3), (1, 1), (1, 2)]
THIRD = 144


def stack_kernel(*refs):
    pieces, stacked_ref, thirds = refs[:7], refs[7], refs[8:]
    for index, piece in enumerate(pieces):
        stacked_ref[index] = piece[...]
    for index, third in enumerate(thirds):
        third[...] = pieces[4 + index][index * THIRD : (index + 1) * THIRD, :]


def hold_kernel(value_ref, earlier_ref, held_ref):
    pass


def hold(value, earlier):
    return pl.pallas_call(
        hold_kernel,
        out_shape=jax.ShapeDtypeStruct(value.shape, value.dtype),
        in_specs=[pl.BlockSpec(memory_space=pl.ANY)] * 2,
        out_specs=pl.BlockSpec(memory_space=pl.ANY),
        input_output_aliases={0: 0},
    )(value, earlier)


GAINS = slice(144, 160)
OUT = 160
IN = 208
DOWN = 352
PACKED = 432


def pack_kernel(qkv_ref, gain_ref, out_ref, in_ref, down_ref, piece_ref):
    for part in range(3):
        cut = slice(part * WIDTH, (part + 1) * WIDTH)
        piece_ref[part * 48 : (part + 1) * 48, :] = qkv_ref[:, cut]
        piece_ref[IN + part * 48 : IN + (part + 1) * 48, :] = in_ref[:, cut]
    piece_ref[GAINS, :] = gain_ref[...]
    piece_ref[OUT : OUT + 48, :] = out_ref[...]
    piece_ref[DOWN : DOWN + 72, :] = down_ref[...]
    piece_ref[DOWN + 72 :, :] = jnp.zeros((8, WIDTH), BF)


def chip_blocks(where_ref):
    x_high, z = where_ref[0], where_ref[1]
    sides = [1 - x_high if turned else x_high for turned, _ in PIECES]
    return [side * 4 + lax.rem(z + step, 4) for side, (_, step) in zip(sides, PIECES)]


def at_rows(block, count):
    return pl.ds(pl.multiple_of(block * count, 16), count)


def place_rows(where_ref, pieces, weight_ref, start, parts):
    core = where_ref[2]
    for index, chip in enumerate(chip_blocks(where_ref)):
        for source, block in ((index, 2 * chip + core), (8 + index, 2 * chip + 1 - core)):
            for part in range(parts):
                rows = slice(start + part * 48, start + (part + 1) * 48)
                columns = slice(part * WIDTH, (part + 1) * WIDTH)
                weight_ref[at_rows(block, 48), columns] = pieces[source, rows, :]


def chosen_columns(core, rows, count):
    row = lax.broadcasted_iota(jnp.int32, (rows, rows // 2), 0)
    column = lax.broadcasted_iota(jnp.int32, (rows, rows // 2), 1)
    wanted = (column // count * 2 + core) * count + lax.rem(column, count)
    return jnp.where(row == wanted, 1.0, 0.0).astype(BF)


def chosen(values, core, count):
    picked = matmul(values, chosen_columns(core, values.shape[1], count))
    return picked.astype(BF)


def matmul(a, b):
    return jnp.dot(a, b, preferred_element_type=F32)


def matmul_turned(a, b):
    return lax.dot_general(a, b, (((1,), (1,)), ((), ())), preferred_element_type=F32)


def turned_matmul(a, b):
    return lax.dot_general(a, b, (((0,), (0,)), ((), ())), preferred_element_type=F32)


def normalize_rows(values):
    centre = values - jnp.mean(values, axis=-1, keepdims=True)
    spread = jnp.mean(centre * centre, axis=-1, keepdims=True)
    row_inverse_scale = lax.rsqrt(spread + norm_epsilon)
    return (centre * row_inverse_scale, row_inverse_scale)


def norm_backward_pass(normalized_gradient, standardized_rows, row_inverse_scale):
    centered_average = jnp.mean(normalized_gradient, axis=-1, keepdims=True)
    projected_average = jnp.mean(normalized_gradient * standardized_rows, axis=-1, keepdims=True)
    return row_inverse_scale * (
        normalized_gradient - centered_average - standardized_rows * projected_average
    )


def lanes_of(shape):
    return lax.broadcasted_iota(jnp.int32, shape, 1)


def turn_halves(values):
    low = lax.rem(lanes_of(values.shape), 64) < 32
    return jnp.where(low, pltpu.roll(values, 96, 1), pltpu.roll(values, 32, 1))


def rotate(vectors, cosine_table, signed_sine):
    return vectors * cosine_table + turn_halves(vectors) * signed_sine


def rotate_back(vectors, cosine_table, signed_sine):
    return vectors * cosine_table + turn_halves(vectors * signed_sine)


def qkv_part(
    where_ref, tokens_ref, above_ref, below_ref, cosine_ref, sine_ref, pieces,
    query_ref, key_ref, value_ref, normed_ref, weight_ref, gain_ref,
):
    place_rows(where_ref, pieces, weight_ref, 0, 3)
    gains = jnp.zeros((16, WIDTH), F32)
    for index in range(16):
        gains = gains + pieces[index, GAINS, :].astype(F32)
    gain_ref[...] = gains
    for source, rows in ((above_ref, slice(0, 64)), (tokens_ref, slice(64, 320)), (below_ref, slice(320, 384))):
        standardized, _ = normalize_rows(source[...].astype(F32))
        normed_ref[rows, :] = (standardized * gains[0:1, :]).astype(BF)
    for pair in range(6):
        cut = slice(pair * 128, (pair + 1) * 128)
        part = matmul(normed_ref[64:320, :], weight_ref[:, cut])
        query_ref[:, cut] = rotate(part, cosine_ref[64:320, :], sine_ref[64:320, :]).astype(BF)
    for pair in range(6):
        cut = slice(pair * 128, (pair + 1) * 128)
        part = matmul(normed_ref[...], weight_ref[:, WIDTH + pair * 128 : WIDTH + (pair + 1) * 128])
        key_ref[:, cut] = rotate(part, cosine_ref[...], sine_ref[...]).astype(BF)
    value_ref[...] = matmul(normed_ref[...], weight_ref[:, 2 * WIDTH :]).astype(BF)


def score_bias(row_segments_ref, column_segments_ref, block):
    rows = slice(block * 128, (block + 1) * 128)
    columns = slice(block * 128, block * 128 + 256)
    row = lax.broadcasted_iota(jnp.int32, (128, 256), 0)
    column = lanes_of((128, 256))
    allowed = (
        (column >= row)
        & (column <= row + 2 * HALF)
        & (row_segments_ref[rows, :] == column_segments_ref[:, columns])
    )
    bias = jnp.where(allowed, 0.0, masked_score)
    return jnp.concatenate([bias, bias], axis=0)


def both_heads(values):
    first = lanes_of(values.shape) < 64
    empty = jnp.zeros_like(values)
    return jnp.concatenate([jnp.where(first, values, empty), jnp.where(first, empty, values)], axis=0)


def joined_heads(values):
    return jnp.where(lanes_of((128, 128)) < 64, values[:128], values[128:])


def attention_part(query_ref, key_ref, value_ref, row_ref, column_ref, context_ref, log_ref):
    logs = jnp.zeros((256, 128), F32)
    lane = lanes_of((256, 128))
    for block in range(2):
        rows = slice(block * 128, (block + 1) * 128)
        span = slice(block * 128, block * 128 + 256)
        bias = score_bias(row_ref, column_ref, block)
        for pair in range(6):
            cut = slice(pair * 128, (pair + 1) * 128)
            queries = both_heads(query_ref[rows, cut])
            scores = matmul_turned(queries, key_ref[span, cut]) * score_scale + bias
            top = jnp.max(scores, axis=-1, keepdims=True)
            exponent = jnp.exp(scores - top)
            total = jnp.sum(exponent, axis=-1, keepdims=True)
            probs = (exponent * (1.0 / total)).astype(BF)
            context_ref[rows, cut] = joined_heads(matmul(probs, value_ref[span, cut])).astype(BF)
            logs = jnp.where(lane == block * 6 + pair, top + jnp.log(total), logs)
    log_ref[...] = logs


GATE_UP = slice(0, 2304)
COTANGENT = slice(2304, 3072)
GRAD_ATTN = slice(3072, 3840)
NORMED = slice(3840, 4224)
CONTEXT = slice(4224, 4608)
MIXED = slice(4608, 5184)
HANDED = 5248


CHUNK = 384


def mlp_part(
    where_ref, tokens_ref, context_ref, cotangent_ref, gain_ref, pieces,
    output_ref, grad_hidden_ref, grad_context_ref, handed_ref, kept_ref,
    out_weight, in_weight, down_weight, mixed_rows,
):
    core = where_ref[2]
    place_rows(where_ref, pieces, out_weight, 0, 1)
    place_rows(where_ref, pieces, in_weight, IN - OUT, 3)
    for index, chip in enumerate(chip_blocks(where_ref)):
        rows = slice(DOWN - OUT, DOWN - OUT + 80)
        here = pieces[index, rows, :].astype(F32)[:72]
        there = pieces[8 + index, rows, :].astype(F32)[:72]
        first = jnp.where(core == 0, here, there)
        second = jnp.where(core == 0, there, here)
        down_weight[at_rows(chip, 144), :] = jnp.concatenate([first, second], axis=0).astype(BF)

    gain = gain_ref[1:2, :]
    hidden = tokens_ref[...].astype(F32) + matmul(context_ref[...], out_weight[...])
    standardized, inverse_scale = normalize_rows(hidden)
    normed = (standardized * gain).astype(BF)
    cotangent = cotangent_ref[...]
    total = hidden
    for chunk in range(1152 // CHUNK):
        cut = slice(chunk * CHUNK, (chunk + 1) * CHUNK)
        second_cut = slice(1152 + chunk * CHUNK, 1152 + (chunk + 1) * CHUNK)
        gate = matmul(normed, in_weight[:, cut])
        up = matmul(normed, in_weight[:, second_cut])
        normal_cdf = 0.5 * (1.0 + lax.erf(gate * root_half))
        normal_pdf = jnp.exp(-0.5 * gate * gate) * density_factor
        activated = gate * normal_cdf
        mixed = (activated * up).astype(BF)
        mixed_rows[:, cut] = mixed
        total = total + matmul(mixed, down_weight[cut, :])
        grad_mixed = matmul_turned(cotangent, down_weight[cut, :])
        handed_ref[:, cut] = (grad_mixed * up * (normal_cdf + gate * normal_pdf)).astype(BF)
        handed_ref[:, second_cut] = (grad_mixed * activated).astype(BF)
    output_ref[...] = total.astype(BF)

    grad_normed = matmul_turned(handed_ref[:, GATE_UP], in_weight[...])
    grad_hidden = cotangent.astype(F32) + norm_backward_pass(
        grad_normed * gain, standardized, inverse_scale
    )
    grad_hidden_ref[...] = grad_hidden
    grad_attn = grad_hidden.astype(BF)
    grad_context_ref[...] = matmul_turned(grad_attn, out_weight[...]).astype(BF)
    handed_ref[:, COTANGENT] = cotangent
    handed_ref[:, GRAD_ATTN] = grad_attn
    handed_ref[:, 5120:] = jnp.zeros((256, 128), BF)
    for target, owner, offset in ((kept_ref, core, 0), (handed_ref, 1 - core, NORMED.start)):
        target[:, offset : offset + 384] = chosen(normed, owner, 48)
        target[:, offset + 384 : offset + 768] = chosen(context_ref[...], owner, 48)
        target[:, offset + 768 : offset + 1344] = chosen(mixed_rows[...], owner, 72)


def forward_kernel(
    where_ref, tokens_ref, above_ref, below_ref, cotangent_ref, cosine_ref, sine_ref,
    row_ref, column_ref, *refs
):
    pieces, rest = refs[:8], refs[8:]
    (
    query_ref, key_ref, value_ref, normed_ref, weight_ref, gain_ref, log_ref,
    output_ref, grad_hidden_ref, grad_context_ref, handed_ref, kept_ref,
    context, out_weight, in_weight, down_weight, mixed_rows, head_rows, tail_rows, arrived,
    ) = rest
    copies = ([], [])

    def bring(source, first, last, part, slot, start):
        target = (head_rows, tail_rows)[part]
        copies[part].append(
            pltpu.make_async_copy(
                source.at[..., pl.ds(first, last - first), :],
                target.at[slot, pl.ds(start, last - first), :],
                arrived.at[len(copies[0]) + len(copies[1])],
            )
        )

    for core in range(2):
        stacked, across, up, down = pieces[4 * core : 4 * core + 4]
        bring(stacked, 0, OUT, 0, pl.ds(8 * core, 7), 0)
        bring(across, 0, THIRD, 0, 8 * core + 7, 0)
        bring(up, 0, OUT - THIRD, 0, 8 * core + 7, THIRD)
        bring(stacked, OUT, PACKED, 1, pl.ds(8 * core, 7), 0)
        bring(up, OUT - THIRD, THIRD, 1, 8 * core + 7, 0)
        bring(down, 0, THIRD, 1, 8 * core + 7, 2 * THIRD - OUT)
    for copy in copies[0] + copies[1]:
        copy.start()
    for copy in copies[0]:
        copy.wait()
    qkv_part(
        where_ref, tokens_ref, above_ref, below_ref, cosine_ref, sine_ref,
        head_rows,
        query_ref, key_ref, value_ref, normed_ref, weight_ref, gain_ref,
    )
    attention_part(query_ref, key_ref, value_ref, row_ref, column_ref, context, log_ref)
    for copy in copies[1]:
        copy.wait()
    mlp_part(
        where_ref, tokens_ref, context, cotangent_ref, gain_ref,
        tail_rows,
        output_ref, grad_hidden_ref, grad_context_ref, handed_ref, kept_ref,
        out_weight, in_weight, down_weight, mixed_rows,
    )


def both_terms(own_left, own_right, arrived_left, arrived_right):
    return turned_matmul(own_left, own_right) + turned_matmul(arrived_left, arrived_right)


def mlp_term_kernel(where_ref, mlp_ref, mlp_kept_ref, mlp_arrived_ref, *rest):
    z_outs, y_outs, (in_terms, end_terms) = rest[:4], rest[4:8], rest[8:]
    z, y = where_ref[1], where_ref[3]
    for part in range(3):
        columns = slice(part * WIDTH, (part + 1) * WIDTH)
        term = both_terms(
            mlp_kept_ref[:, 0:384],
            mlp_ref[:, columns],
            mlp_arrived_ref[:, NORMED],
            mlp_arrived_ref[:, columns],
        )
        in_terms[:, part * 48 : (part + 1) * 48, :] = term.reshape(8, 48, WIDTH).astype(BF)
    out_term = both_terms(
        mlp_kept_ref[:, 384:768],
        mlp_ref[:, GRAD_ATTN],
        mlp_arrived_ref[:, CONTEXT],
        mlp_arrived_ref[:, GRAD_ATTN],
    )
    down_term = both_terms(
        mlp_kept_ref[:, 768:1344],
        mlp_ref[:, COTANGENT],
        mlp_arrived_ref[:, MIXED],
        mlp_arrived_ref[:, COTANGENT],
    )
    end_terms[...] = jnp.concatenate(
        [
            out_term.reshape(8, 48, WIDTH),
            down_term.reshape(8, 72, WIDTH),
            jnp.zeros((8, 8, WIDTH), F32),
        ],
        axis=1,
    ).astype(BF)
    for step in range(4):
        for side in range(2):
            z_outs[step][side] = in_terms[side * 4 + lax.rem(z + step, 4)]
        quarter = lax.rem(y + step, 4)
        y_outs[step][...] = end_terms[:, pl.ds(pl.multiple_of(quarter * 32, 32), 32), :]


def qkv_term_kernel(where_ref, qkv_ref, qkv_kept_ref, qkv_arrived_ref, own_ref, sent_ref, terms):
    x_high = where_ref[0]
    for part in range(3):
        columns = slice(part * WIDTH, (part + 1) * WIDTH)
        term = both_terms(
            qkv_kept_ref[...],
            qkv_ref[:, columns],
            qkv_arrived_ref[:, 3 * WIDTH :],
            qkv_arrived_ref[:, columns],
        )
        terms[:, part * 48 : (part + 1) * 48, :] = term.reshape(8, 48, WIDTH).astype(BF)
    for out, side in ((own_ref, x_high), (sent_ref, 1 - x_high)):
        for block in range(4):
            out[block] = terms[side * 4 + block]


def attention_backward_kernel(
    where_ref, query_ref, key_ref, value_ref, grad_context_ref, row_ref, column_ref, log_ref,
    cosine_ref, sine_ref, normed_ref,
    handed_ref, kept_ref, above_ref, below_ref,
    key_sum, value_sum,
):
    core = where_ref[2]
    handed_ref[0:64, 0:WIDTH] = jnp.zeros((64, WIDTH), BF)
    handed_ref[320:384, 0:WIDTH] = jnp.zeros((64, WIDTH), BF)
    for block in range(2):
        rows = slice(block * 128, (block + 1) * 128)
        span = slice(block * 128, block * 128 + 256)
        bias = score_bias(row_ref, column_ref, block)
        for pair in range(6):
            cut = slice(pair * 128, (pair + 1) * 128)
            queries = both_heads(query_ref[rows, cut])
            grads = both_heads(grad_context_ref[rows, cut])
            keys = key_ref[span, cut]
            scores = matmul_turned(queries, keys) * score_scale + bias
            index = block * 6 + pair
            probs = jnp.exp(scores - log_ref[:, index : index + 1])
            grad_probs = matmul_turned(grads, value_ref[span, cut])
            inner = jnp.sum(probs * grad_probs, axis=-1, keepdims=True)
            grad_scores = (probs * (grad_probs - inner)).astype(BF)
            own = joined_heads(matmul(grad_scores, keys)) * score_scale
            turned = slice(64 + block * 128, 64 + (block + 1) * 128)
            handed_ref[turned, cut] = rotate_back(
                own, cosine_ref[turned, :], sine_ref[turned, :]
            ).astype(BF)
            key_part = turned_matmul(grad_scores, queries) * score_scale
            value_part = turned_matmul(probs.astype(BF), grads)
            if block == 0:
                key_sum[0:256, cut] = key_part
                value_sum[0:256, cut] = value_part
            else:
                key_sum[128:256, cut] += key_part[:128]
                value_sum[128:256, cut] += value_part[:128]
                key_sum[256:384, cut] = key_part[128:]
                value_sum[256:384, cut] = value_part[128:]
    for pair in range(6):
        cut = slice(pair * 128, (pair + 1) * 128)
        handed_ref[:, WIDTH + pair * 128 : WIDTH + (pair + 1) * 128] = rotate_back(
            key_sum[:, cut], cosine_ref[...], sine_ref[...]
        ).astype(BF)
    handed_ref[:, 2 * WIDTH : 3 * WIDTH] = value_sum[...].astype(BF)
    handed_ref[:, 3 * WIDTH :] = chosen(normed_ref[...], 1 - core, 48)
    kept_ref[...] = chosen(normed_ref[...], core, 48)
    above_ref[...] = handed_ref[320:384, WIDTH : 3 * WIDTH]
    below_ref[...] = handed_ref[0:64, WIDTH : 3 * WIDTH]


def token_grad_kernel(
    tokens_ref, grads_ref, above_ref, below_ref,
    weight_ref, gain_ref, grad_hidden_ref, grad_tokens_ref,
):
    total = matmul_turned(grads_ref[64:320, :WIDTH], weight_ref[:, :WIDTH])
    for part in (1, 2):
        cut = slice((part - 1) * WIDTH, part * WIDTH)
        own = slice(part * WIDTH, (part + 1) * WIDTH)
        head = grads_ref[64:128, own].astype(F32) + above_ref[:, cut].astype(F32)
        tail = grads_ref[256:320, own].astype(F32) + below_ref[:, cut].astype(F32)
        rows = jnp.concatenate([head.astype(BF), grads_ref[128:256, own], tail.astype(BF)], axis=0)
        total = total + matmul_turned(rows, weight_ref[:, part * WIDTH : (part + 1) * WIDTH])
    standardized, inverse_scale = normalize_rows(tokens_ref[...].astype(F32))
    grad_tokens_ref[...] = (
        grad_hidden_ref[...]
        + norm_backward_pass(total * gain_ref[0:1, :], standardized, inverse_scale)
    ).astype(BF)


def call(kernel, arrays, outs, scratch=(), where=None, read=(), after=(), flops=0):
    first = [] if where is None else [pl.BlockSpec(memory_space=pltpu.SMEM)]
    in_vmem = pl.BlockSpec(memory_space=pltpu.VMEM)
    begin = len(first) + len(arrays) + len(read)

    def body(*refs):
        kernel(*refs[:begin], *refs[begin + len(after) :])

    return pl.pallas_call(
        body,
        out_shape=[jax.ShapeDtypeStruct(shape, kind) for shape, kind in outs],
        in_specs=first
        + [in_vmem] * len(arrays)
        + [pl.BlockSpec(memory_space=pl.ANY)] * (len(read) + len(after)),
        out_specs=[in_vmem] * len(outs),
        scratch_shapes=[
            pltpu.VMEM(shape, kind) if kind else pltpu.SemaphoreType.DMA(shape)
            for shape, kind in scratch
        ],
        compiler_params=pltpu.CompilerParams(vmem_limit_bytes=56 * 1024 * 1024),
        cost_estimate=pl.CostEstimate(flops=flops, bytes_accessed=0, transcendentals=0),
    )(*([] if where is None else [where]), *arrays, *read, *after)


def sum_of(refs, *index):
    total = refs[0][index].astype(F32)
    for ref in refs[1:]:
        total = total + ref[index].astype(F32)
    return total


def second_kernel(where_ref, *refs):
    z_refs, x_refs, y_refs, outs = refs[:4], refs[4:6], refs[6:10], refs[10:]
    x_high, z = where_ref[0], where_ref[1]
    for out, side in zip(outs[:2], (x_high, 1 - x_high)):
        out[0:144, :] = sum_of(z_refs, side).astype(BF)
        for block in range(4):
            rows = slice(144 + block * 32, 144 + (block + 1) * 32)
            out[rows, :] = sum_of(y_refs, side * 4 + block).astype(BF)
    for step in range(4):
        outs[2 + step][...] = sum_of(x_refs, lax.rem(z + step, 4)).astype(BF)


def third_kernel(where_ref, *refs):
    x_refs, z_refs, y_outs, z_outs, blocks, ends = refs[:2], refs[2:6], refs[6:10], refs[10:14], refs[14], refs[15]
    z, y = where_ref[1], where_ref[3]
    blocks[0:144, :] = sum_of(x_refs, slice(0, 144))
    blocks[144:288, :] = sum_of(z_refs)
    ends[...] = sum_of(x_refs, slice(144, 272)).reshape(4, 32, WIDTH)
    for step in range(4):
        rows = pl.ds(pl.multiple_of(lax.rem(y + step, 4) * 72, 8), 72)
        y_outs[step][...] = blocks[rows, :].astype(BF)
        z_outs[step][...] = ends[lax.rem(z + step, 4)].astype(BF)


def fourth_kernel(*refs):
    refs[8][...] = jnp.concatenate([sum_of(refs[:4]), sum_of(refs[4:8])], axis=0).astype(BF)


def twin_sum_kernel(*refs):
    refs[2][...] = sum_of(refs[:2]).astype(BF)


def final_weight(total, weight_ref, gain_ref, grad_ref, gain_grad_ref):
    dots = jnp.zeros((48, 128), F32)
    for part in range(3):
        cut = slice(part * WIDTH, (part + 1) * WIDTH)
        grad = total[part * 48 : (part + 1) * 48, :]
        grad_ref[:, cut] = grad
        products = weight_ref[:, cut].astype(F32) * grad
        for start in range(0, WIDTH, 128):
            dots = dots + products[:, start : start + 128]
    gain_grad_ref[...] = jnp.sum(dots.T, axis=0, keepdims=True) / gain_ref[...].astype(F32)


def final_kernel(
    where_ref, a, b, c, d, w_qkv_ref, gain1_ref, w_in_ref, gain2_ref,
    qkv_ref, qkv_gain_ref, in_ref, in_gain_ref, out_ref, down_ref, blocks, ends,
):
    y = where_ref[3]
    for step, part in enumerate((a, b, c, d)):
        quarter = lax.rem(y + step, 4)
        values = part[...].astype(F32)
        blocks[pl.ds(pl.multiple_of(quarter * 72, 8), 72), :] = values[:72]
        ends[pl.ds(pl.multiple_of(quarter * 32, 8), 32), :] = values[72:]
    final_weight(blocks[0:144, :], w_in_ref, gain2_ref, in_ref, in_gain_ref)
    final_weight(blocks[144:288, :], w_qkv_ref, gain1_ref, qkv_ref, qkv_gain_ref)
    out_ref[...] = ends[0:48, :]
    down_ref[...] = ends[48:120, :]


STEPS = (1, 2, 3)


def angles(position):
    fractions = jnp.arange(0, HEAD, 2).astype(F32) / HEAD
    inverse = jnp.exp(-math.log(10000.0) * fractions)
    phases = position.astype(F32)[:, None] * inverse[None, :]
    cosine, sine = jnp.cos(phases), jnp.sin(phases)
    return (
        jnp.concatenate([cosine] * 4, axis=1),
        jnp.concatenate([-sine, sine, -sine, sine], axis=1),
    )


def neighbours(count, step):
    return [(i, i + step) for i in range(count) if 0 <= i + step < count]


def shards(
    tokens, segment_ids, norm1_gain, w_qkv, w_attn_out, norm2_gain, w_in, w_mlp_out, cotangent
):
    row_count = tokens.shape[0]
    key_span = row_count + 2 * HALF
    at = place()
    where = jnp.stack([at["x_high"], at["z"], at["core"], at["y"]]).astype(jnp.int32)
    shard_place = at["shard"]

    gains = jnp.stack([norm1_gain, norm2_gain])
    spread_gains = lax.dynamic_update_slice(
        jnp.zeros((16, WIDTH), BF), gains, (jnp.zeros((), jnp.int32), shard_place * 48)
    )
    (piece,) = call(
        pack_kernel, [w_qkv, spread_gains, w_attn_out, w_in, w_mlp_out], [((PACKED, WIDTH), BF)]
    )
    own = {(0, 0): piece}
    own[1, 0] = send(piece, ACROSS_X)
    own[0, 3] = send(piece, Z_STEP[1])
    own[0, 1] = send(piece, Z_STEP[3])
    own[1, 1] = send(own[0, 1], ACROSS_X)
    own[1, 3] = send(own[1, 0], Z_STEP[1])
    own[0, 2] = send(own[0, 1], Z_STEP[3])
    tokens_above = lax.ppermute(tokens[row_count - HALF :], "shard", neighbours(16, 1))
    tokens_below = lax.ppermute(tokens[:HALF], "shard", neighbours(16, -1))

    first_row = shard_place * row_count
    seq_segs = segment_ids[0]
    segs_pad = jnp.pad(seq_segs, (HALF, HALF), constant_values=-1)
    key_segs = lax.dynamic_slice_in_dim(segs_pad, first_row, key_span, 0)
    own_segs = key_segs[HALF : HALF + row_count]
    earlier = jnp.sum((seq_segs[None, :] < key_segs[:, None]).astype(jnp.int32), axis=1)
    position = jnp.arange(key_span, dtype=jnp.int32) - HALF + first_row - earlier
    cosine_table, signed_sine = angles(position)
    row_segs, column_segs = own_segs[:, None], key_segs[None, :]

    square = (row_count, WIDTH)
    wide = (key_span, WIDTH)
    stacked, *thirds = call(
        stack_kernel,
        [own[key] for key in ((0, 0), (1, 0), (0, 3), (0, 1), (0, 2), (1, 3), (1, 1))],
        [((7, PACKED, WIDTH), BF)] + [((THIRD, WIDTH), BF)] * 3,
        after=[tokens_above, tokens_below, cosine_table, signed_sine, row_segs, column_segs, where],
    )
    pieces = [stacked] + [
        send(part, route) for part, route in zip(thirds, (ACROSS_X, Z_STEP[1], Z_STEP[3]))
    ]
    pieces += [send(value, OTHER_CORE) for value in pieces]
    (
        queries, keys, values, first_normed, wqkv_all, gain_table, log_total,
        output, grad_hidden, grad_context, mlp_handed, mlp_kept,
    ) = call(
        forward_kernel,
        [tokens, tokens_above, tokens_below, cotangent, cosine_table, signed_sine]
        + [row_segs, column_segs],
        [(square, BF), (wide, BF), (wide, BF), (wide, BF), ((WIDTH, 3 * WIDTH), BF)]
        + [((16, WIDTH), F32), ((256, 128), F32)]
        + [(square, BF), (square, F32), (square, BF), ((256, HANDED), BF), ((256, 1344), BF)],
        scratch=[
            (square, BF),
            ((WIDTH, WIDTH), BF),
            ((WIDTH, 3 * WIDTH), BF),
            ((1152, WIDTH), BF),
            ((row_count, 1152), BF),
            ((16, OUT, WIDTH), BF),
            ((16, PACKED - OUT, WIDTH), BF),
            ((12,), None),
        ],
        where=where,
        read=pieces,
    )
    mlp_arrived = send(mlp_handed, OTHER_CORE)
    qkv_handed, qkv_kept, last_grads, first_grads = call(
        attention_backward_kernel,
        [queries, keys, values, grad_context, row_segs, column_segs, log_total]
        + [cosine_table, signed_sine, first_normed],
        [((key_span, 3 * WIDTH + 384), BF), ((key_span, 384), BF)] + [((HALF, 2 * WIDTH), BF)] * 2,
        scratch=[(wide, F32), (wide, F32)],
        where=where,
    )
    qkv_arrived = send(qkv_handed, OTHER_CORE)
    grads_above = lax.ppermute(last_grads, "shard", neighbours(16, 1))
    grads_below = lax.ppermute(first_grads, "shard", neighbours(16, -1))
    stage = call(
        mlp_term_kernel,
        [mlp_handed, mlp_kept, mlp_arrived],
        [((2, 144, WIDTH), BF)] * 4 + [((8, 32, WIDTH), BF)] * 4,
        scratch=[((8, 144, WIDTH), BF), ((8, 128, WIDTH), BF)],
        where=where,
        after=[qkv_handed],
        flops=40_000_000_000,
    )
    z_parts, y_parts = stage[:4], stage[4:]
    x_parts = call(
        qkv_term_kernel,
        [qkv_handed, qkv_kept, qkv_arrived],
        [((4, 144, WIDTH), BF)] * 2,
        scratch=[((8, 144, WIDTH), BF)],
        where=where,
        after=[grads_above, grads_below, z_parts[0]],
        flops=40_000_000_000,
    )
    x_arrived = send(x_parts[1], ACROSS_X)
    z_arrived = [send(z_parts[step], Z_STEP[step]) for step in STEPS]
    y_arrived = [send(y_parts[1], Y_STEP[1])]
    y_arrived += [send(hold(y_parts[step], y_arrived[0]), Y_STEP[step]) for step in (3, 2)]
    (grad_tokens,) = call(
        token_grad_kernel,
        [tokens, qkv_handed, grads_above, grads_below, wqkv_all, gain_table, grad_hidden],
        [(square, BF)],
        after=[x_parts[0]],
        flops=40_000_000_000,
    )
    stage = call(
        second_kernel,
        [z_parts[0], *z_arrived, x_parts[0], x_arrived, y_parts[0], *y_arrived],
        [((272, WIDTH), BF)] * 2 + [((144, WIDTH), BF)] * 4,
        where=where,
        after=[grad_tokens],
    )
    x_arrived = send(stage[1], ACROSS_X)
    z_arrived = [send(stage[2 + step], Z_STEP[step]) for step in STEPS]
    stage = call(
        third_kernel,
        [stage[0], x_arrived, stage[2], *z_arrived],
        [((72, WIDTH), BF)] * 4 + [((32, WIDTH), BF)] * 4,
        scratch=[((288, WIDTH), F32), ((4, 32, WIDTH), F32)],
        where=where,
    )
    y_arrived = [send(stage[step], Y_STEP[step]) for step in STEPS]
    z_arrived = [send(stage[4 + step], Z_STEP[step]) for step in STEPS]
    part = [((104, WIDTH), BF)]
    (total,) = call(fourth_kernel, [stage[0], *y_arrived, stage[4], *z_arrived], part)
    (total,) = call(twin_sum_kernel, [total, send(total, TWIN_X)], part)
    quarters = [total] + [send(total, Y_STEP[4 - step]) for step in STEPS]
    columns = (48, 3 * WIDTH)
    grad_w_qkv, gain1, grad_w_in, gain2, grad_w_out, grad_w_down = call(
        final_kernel,
        [*quarters, w_qkv, norm1_gain[None, :], w_in, norm2_gain[None, :]],
        [(columns, F32), ((1, 48), F32), (columns, F32), ((1, 48), F32)]
        + [((48, WIDTH), F32), ((72, WIDTH), F32)],
        scratch=[((288, WIDTH), F32), ((128, WIDTH), F32)],
        where=where,
    )
    return (
        output, grad_tokens, gain1[0], grad_w_qkv, grad_w_out, gain2[0], grad_w_in, grad_w_down
    )


def solution(mesh):
    return jax.shard_map(
        shards,
        mesh=mesh,
        in_specs=(
            P(("rep", "shard"), None),
            P("rep", None),
            P("shard"),
            P("shard", None),
            P("shard", None),
            P("shard"),
            P("shard", None),
            P("shard", None),
            P(("rep", "shard"), None),
        ),
        out_specs=(
            P(("rep", "shard"), None),
            P(("rep", "shard"), None),
            P("shard"),
            P("shard", None),
            P("shard", None),
            P("shard"),
            P("shard", None),
            P("shard", None),
        ),
        check_vma=False,
    )
```

```python
import functools
import math

import jax
import jax.numpy as jnp
from jax import lax
from jax.experimental import pallas as pl
from jax.experimental.pallas import tpu as pltpu
from jax.sharding import PartitionSpec as P

HEADS = 12
HEAD = 64
HALF = 64
WIDTH = 768
AXES = ("rep", "shard")
BF = jnp.bfloat16
F32 = jnp.float32

norm_epsilon = 1e-05
masked_score = -1e30
root_half = 0.7071067811865476
density_factor = 0.3989422804014327
score_scale = 0.125


def coordinates(device):
    rep, shard = divmod(device, 16)
    x_low, y = divmod(rep, 4)
    x_high, rest = divmod(shard, 8)
    z, core = divmod(rest, 2)
    return x_high * 2 + x_low, y, z, core


def number(x, y, z, core):
    return ((x % 2) * 4 + y) * 16 + (x // 2) * 8 + z * 2 + core


def pairs(move):
    return [(device, number(*move(*coordinates(device)))) for device in range(128)]


def along_z(step):
    return pairs(lambda x, y, z, core: (x, y, (z + step) % 4, core))


def along_y(step):
    return pairs(lambda x, y, z, core: (x, (y + step) % 4, z, core))


OTHER_CORE = pairs(lambda x, y, z, core: (x, y, z, 1 - core))
ACROSS_X = pairs(lambda x, y, z, core: (3 - x, y, z, core))
TWIN_X = pairs(lambda x, y, z, core: (x ^ 1, y, z, core))
Z_STEP = {step: along_z(step) for step in (1, 2, 3)}
Y_STEP = {step: along_y(step) for step in (1, 2, 3)}


def send(value, route):
    return lax.ppermute(value, AXES, route)


def place():
    shard = lax.axis_index("shard")
    rep = lax.axis_index("rep")
    return {
        "x_high": shard // 8,
        "z": (shard // 2) % 4,
        "core": shard % 2,
        "x_low": rep // 4,
        "y": rep % 4,
        "shard": shard,
    }


PIECES = [(0, 0), (1, 0), (0, 3), (0, 1), (0, 2), (1, 3), (1, 1), (1, 2)]
THIRD = 144


def stack_kernel(*refs):
    pieces, stacked_ref, thirds = refs[:7], refs[7], refs[8:]
    for index, piece in enumerate(pieces):
        stacked_ref[index] = piece[...]
    for index, third in enumerate(thirds):
        third[...] = pieces[4 + index][index * THIRD : (index + 1) * THIRD, :]


def hold_kernel(value_ref, earlier_ref, held_ref):
    pass


def hold(value, earlier):
    return pl.pallas_call(
        hold_kernel,
        out_shape=jax.ShapeDtypeStruct(value.shape, value.dtype),
        in_specs=[pl.BlockSpec(memory_space=pl.ANY)] * 2,
        out_specs=pl.BlockSpec(memory_space=pl.ANY),
        input_output_aliases={0: 0},
    )(value, earlier)


GAINS = slice(144, 160)
OUT = 160
IN = 208
DOWN = 352
PACKED = 432


def pack_kernel(
    qkv_ref, gain1_ref, gain2_ref, out_ref, in_ref, down_ref, piece_ref, gain1, gain2, down, done
):
    moves = [(gain1_ref, gain1), (gain2_ref, gain2), (down_ref, down)]
    moves.append((out_ref, piece_ref.at[pl.ds(OUT, 48), :]))
    for part in range(3):
        cut = pl.ds(part * WIDTH, WIDTH)
        moves.append((qkv_ref.at[:, cut], piece_ref.at[pl.ds(part * 48, 48), :]))
        moves.append((in_ref.at[:, cut], piece_ref.at[pl.ds(IN + part * 48, 48), :]))
    copies = [
        pltpu.make_async_copy(source, target, done.at[index])
        for index, (source, target) in enumerate(moves)
    ]
    for copy in copies:
        copy.start()
    first = lax.axis_index("shard") * 48
    row = lax.broadcasted_iota(jnp.int32, (48, WIDTH), 0)
    own_lanes = jnp.where(lanes_of((48, WIDTH)) == row + first, 1.0, 0.0).astype(BF)
    which = lax.broadcasted_iota(jnp.int32, (16, 48), 0)
    for copy in copies[:3]:
        copy.wait()
    gains = jnp.where(
        which == 0,
        gain1[...].astype(F32),
        jnp.where(which == 1, gain2[...].astype(F32), 0.0),
    )
    piece_ref[GAINS, :] = matmul(gains.astype(BF), own_lanes).astype(BF)
    padded = jnp.concatenate([down[...].astype(F32), jnp.zeros((8, WIDTH), F32)], axis=0)
    piece_ref[DOWN:, :] = padded.astype(BF)
    for copy in copies[3:]:
        copy.wait()


def chip_blocks(where_ref):
    x_high, z = where_ref[0], where_ref[1]
    sides = [1 - x_high if turned else x_high for turned, _ in PIECES]
    return [side * 4 + lax.rem(z + step, 4) for side, (_, step) in zip(sides, PIECES)]


def at_rows(block, count):
    return pl.ds(pl.multiple_of(block * count, 16), count)


def packed_rows(pieces, index, first, last):
    core, number_of = divmod(index, 8)
    stacked, *thirds = pieces[4 * core : 4 * core + 4]
    if number_of < 7:
        return stacked[number_of, first:last, :]
    found = []
    for position, third in enumerate(thirds):
        begin, end = max(first - position * THIRD, 0), min(last - position * THIRD, THIRD)
        if begin < end:
            found.append(third[begin:end, :])
    return found[0] if len(found) == 1 else jnp.concatenate(found, axis=0)


def place_rows(where_ref, pieces, weight_ref, start, parts):
    core = where_ref[2]
    for index, chip in enumerate(chip_blocks(where_ref)):
        for source, block in ((index, 2 * chip + core), (8 + index, 2 * chip + 1 - core)):
            for part in range(parts):
                columns = slice(part * WIDTH, (part + 1) * WIDTH)
                weight_ref[at_rows(block, 48), columns] = packed_rows(
                    pieces, source, start + part * 48, start + (part + 1) * 48
                )


def chosen_columns(core, rows, count):
    row = lax.broadcasted_iota(jnp.int32, (rows, rows // 2), 0)
    column = lax.broadcasted_iota(jnp.int32, (rows, rows // 2), 1)
    wanted = (column // count * 2 + core) * count + lax.rem(column, count)
    return jnp.where(row == wanted, 1.0, 0.0).astype(BF)


def chosen(values, core, count):
    picked = matmul(values, chosen_columns(core, values.shape[1], count))
    return picked.astype(BF)


def matmul(a, b):
    return jnp.dot(a, b, preferred_element_type=F32)


def matmul_turned(a, b):
    return lax.dot_general(a, b, (((1,), (1,)), ((), ())), preferred_element_type=F32)


def turned_matmul(a, b):
    return lax.dot_general(a, b, (((0,), (0,)), ((), ())), preferred_element_type=F32)


def normalize_rows(values):
    centre = values - jnp.mean(values, axis=-1, keepdims=True)
    spread = jnp.mean(centre * centre, axis=-1, keepdims=True)
    row_inverse_scale = lax.rsqrt(spread + norm_epsilon)
    return (centre * row_inverse_scale, row_inverse_scale)


def norm_backward_pass(normalized_gradient, standardized_rows, row_inverse_scale):
    centered_average = jnp.mean(normalized_gradient, axis=-1, keepdims=True)
    projected_average = jnp.mean(normalized_gradient * standardized_rows, axis=-1, keepdims=True)
    return row_inverse_scale * (
        normalized_gradient - centered_average - standardized_rows * projected_average
    )


def lanes_of(shape):
    return lax.broadcasted_iota(jnp.int32, shape, 1)


def turn_halves(values):
    low = lax.rem(lanes_of(values.shape), 64) < 32
    return jnp.where(low, pltpu.roll(values, 96, 1), pltpu.roll(values, 32, 1))


def rotate(vectors, cosine_table, signed_sine):
    return vectors * cosine_table + turn_halves(vectors) * signed_sine


def rotate_back(vectors, cosine_table, signed_sine):
    return vectors * cosine_table + turn_halves(vectors * signed_sine)


def qkv_part(
    where_ref, tokens_ref, above_ref, below_ref, cosine_ref, sine_ref, pieces,
    query_ref, key_ref, value_ref, normed_ref, weight_ref, gain_ref,
):
    place_rows(where_ref, pieces, weight_ref, 0, 3)
    gains = jnp.zeros((16, WIDTH), F32)
    for index in range(16):
        gains = gains + packed_rows(pieces, index, GAINS.start, GAINS.stop).astype(F32)
    gain_ref[...] = gains
    for source, rows in ((above_ref, slice(0, 64)), (tokens_ref, slice(64, 320)), (below_ref, slice(320, 384))):
        standardized, _ = normalize_rows(source[...].astype(F32))
        normed_ref[rows, :] = (standardized * gains[0:1, :]).astype(BF)
    for wide in range(0, WIDTH, 256):
        query = matmul(normed_ref[64:320, :], weight_ref[:, wide : wide + 256])
        key = matmul(normed_ref[...], weight_ref[:, WIDTH + wide : WIDTH + wide + 256])
        for half in range(0, 256, 128):
            cut, here = slice(wide + half, wide + half + 128), slice(half, half + 128)
            query_ref[:, cut] = rotate(
                query[:, here], cosine_ref[64:320, :], sine_ref[64:320, :]
            ).astype(BF)
            key_ref[:, cut] = rotate(key[:, here], cosine_ref[...], sine_ref[...]).astype(BF)
    value_ref[...] = matmul(normed_ref[...], weight_ref[:, 2 * WIDTH :]).astype(BF)


def score_bias(row_segments_ref, column_segments_ref, block):
    rows = slice(block * 128, (block + 1) * 128)
    columns = slice(block * 128, block * 128 + 256)
    row = lax.broadcasted_iota(jnp.int32, (128, 256), 0)
    column = lanes_of((128, 256))
    allowed = (
        (column >= row)
        & (column <= row + 2 * HALF)
        & (row_segments_ref[rows, :] == column_segments_ref[:, columns])
    )
    bias = jnp.where(allowed, 0.0, masked_score)
    return jnp.concatenate([bias, bias], axis=0)


def both_heads(values):
    first = lanes_of(values.shape) < 64
    empty = jnp.zeros_like(values)
    return jnp.concatenate([jnp.where(first, values, empty), jnp.where(first, empty, values)], axis=0)


def joined_heads(values):
    return jnp.where(lanes_of((128, 128)) < 64, values[:128], values[128:])


def attention_part(query_ref, key_ref, value_ref, row_ref, column_ref, context_ref, log_ref):
    logs = jnp.zeros((256, 128), F32)
    lane = lanes_of((256, 128))
    for block in range(2):
        rows = slice(block * 128, (block + 1) * 128)
        span = slice(block * 128, block * 128 + 256)
        bias = score_bias(row_ref, column_ref, block)
        for pair in range(6):
            cut = slice(pair * 128, (pair + 1) * 128)
            queries = both_heads(query_ref[rows, cut])
            scores = matmul_turned(queries, key_ref[span, cut]) * score_scale + bias
            top = jnp.max(scores, axis=-1, keepdims=True)
            exponent = jnp.exp(scores - top)
            total = jnp.sum(exponent, axis=-1, keepdims=True)
            probs = (exponent * (1.0 / total)).astype(BF)
            context_ref[rows, cut] = joined_heads(matmul(probs, value_ref[span, cut])).astype(BF)
            logs = jnp.where(lane == block * 6 + pair, top + jnp.log(total), logs)
    log_ref[...] = logs


GATE_UP = slice(0, 2304)
COTANGENT = slice(2304, 3072)
GRAD_ATTN = slice(3072, 3840)
NORMED = slice(3840, 4224)
CONTEXT = slice(4224, 4608)
MIXED = slice(4608, 5184)
HANDED = 5248


CHUNK = 1152


def mlp_part(
    where_ref, tokens_ref, context_ref, cotangent_ref, gain_ref, pieces,
    output_ref, grad_hidden_ref, grad_context_ref, handed_ref, kept_ref,
    out_weight, in_weight, down_weight, mixed_rows, hidden_done,
):
    core = where_ref[2]
    place_rows(where_ref, pieces, out_weight, OUT, 1)
    place_rows(where_ref, pieces, in_weight, IN, 3)
    for index, chip in enumerate(chip_blocks(where_ref)):
        here = packed_rows(pieces, index, DOWN, PACKED).astype(F32)[:72]
        there = packed_rows(pieces, 8 + index, DOWN, PACKED).astype(F32)[:72]
        first = jnp.where(core == 0, here, there)
        second = jnp.where(core == 0, there, here)
        down_weight[at_rows(chip, 144), :] = jnp.concatenate([first, second], axis=0).astype(BF)

    gain = gain_ref[1:2, :]
    hidden = tokens_ref[...].astype(F32) + matmul(context_ref[...], out_weight[...])
    standardized, inverse_scale = normalize_rows(hidden)
    normed = (standardized * gain).astype(BF)
    cotangent = cotangent_ref[...]
    total = hidden
    for chunk in range(1152 // CHUNK):
        cut = slice(chunk * CHUNK, (chunk + 1) * CHUNK)
        second_cut = slice(1152 + chunk * CHUNK, 1152 + (chunk + 1) * CHUNK)
        gate = matmul(normed, in_weight[:, cut])
        up = matmul(normed, in_weight[:, second_cut])
        normal_cdf = 0.5 * (1.0 + lax.erf(gate * root_half))
        normal_pdf = jnp.exp(-0.5 * gate * gate) * density_factor
        activated = gate * normal_cdf
        mixed = (activated * up).astype(BF)
        mixed_rows[:, cut] = mixed
        total = total + matmul(mixed, down_weight[cut, :])
        grad_mixed = matmul_turned(cotangent, down_weight[cut, :])
        handed_ref[:, cut] = (grad_mixed * up * (normal_cdf + gate * normal_pdf)).astype(BF)
        handed_ref[:, second_cut] = (grad_mixed * activated).astype(BF)
    output_ref[...] = total.astype(BF)

    grad_normed = matmul_turned(handed_ref[:, GATE_UP], in_weight[...])
    grad_hidden = cotangent.astype(F32) + norm_backward_pass(
        grad_normed * gain, standardized, inverse_scale
    )
    grad_hidden_ref[...] = grad_hidden
    hidden_done()
    grad_attn = grad_hidden.astype(BF)
    grad_context_ref[...] = matmul_turned(grad_attn, out_weight[...]).astype(BF)
    handed_ref[:, COTANGENT] = cotangent
    handed_ref[:, GRAD_ATTN] = grad_attn
    handed_ref[:, 5120:] = jnp.zeros((256, 128), BF)
    for target, owner, offset in ((kept_ref, core, 0), (handed_ref, 1 - core, NORMED.start)):
        target[:, offset : offset + 384] = chosen(normed, owner, 48)
        target[:, offset + 384 : offset + 768] = chosen(context_ref[...], owner, 48)
        target[:, offset + 768 : offset + 1344] = chosen(mixed_rows[...], owner, 72)


def forward_kernel(
    where_ref, tokens_ref, above_ref, below_ref, cotangent_ref, cosine_ref, sine_ref,
    row_ref, column_ref, *refs
):
    pieces, rest = refs[:8], refs[8:]
    (
    query_ref, key_ref, value_ref, normed_ref, far_weight_ref, far_gain_ref, log_ref,
    output_ref, far_hidden_ref, grad_context_ref, handed_ref, kept_ref,
    context, weight, gain_ref, grad_hidden_ref, out_weight, in_weight, down_weight, mixed_rows,
    written,
    ) = rest
    qkv_part(
        where_ref, tokens_ref, above_ref, below_ref, cosine_ref, sine_ref, pieces,
        query_ref, key_ref, value_ref, normed_ref, weight, gain_ref,
    )
    copies = [
        pltpu.make_async_copy(source, target, written.at[index])
        for index, (source, target) in enumerate(
            ((weight, far_weight_ref), (gain_ref, far_gain_ref), (grad_hidden_ref, far_hidden_ref))
        )
    ]
    copies[0].start()
    copies[1].start()
    attention_part(query_ref, key_ref, value_ref, row_ref, column_ref, context, log_ref)
    mlp_part(
        where_ref, tokens_ref, context, cotangent_ref, gain_ref, pieces,
        output_ref, grad_hidden_ref, grad_context_ref, handed_ref, kept_ref,
        out_weight, in_weight, down_weight, mixed_rows, copies[2].start,
    )
    for copy in copies:
        copy.wait()


def both_terms(own_left, own_right, arrived_left, arrived_right):
    return turned_matmul(own_left, own_right) + turned_matmul(arrived_left, arrived_right)


def mlp_term_kernel(where_ref, mlp_ref, mlp_kept_ref, mlp_arrived_ref, *rest):
    z_outs, y_outs, (in_terms, end_terms) = rest[:4], rest[4:8], rest[8:]
    z, y = where_ref[1], where_ref[3]
    for part in range(3):
        columns = slice(part * WIDTH, (part + 1) * WIDTH)
        term = both_terms(
            mlp_kept_ref[:, 0:384],
            mlp_ref[:, columns],
            mlp_arrived_ref[:, NORMED],
            mlp_arrived_ref[:, columns],
        )
        in_terms[:, part * 48 : (part + 1) * 48, :] = term.reshape(8, 48, WIDTH).astype(BF)
    out_term = both_terms(
        mlp_kept_ref[:, 384:768],
        mlp_ref[:, GRAD_ATTN],
        mlp_arrived_ref[:, CONTEXT],
        mlp_arrived_ref[:, GRAD_ATTN],
    )
    down_term = both_terms(
        mlp_kept_ref[:, 768:1344],
        mlp_ref[:, COTANGENT],
        mlp_arrived_ref[:, MIXED],
        mlp_arrived_ref[:, COTANGENT],
    )
    end_terms[...] = jnp.concatenate(
        [
            out_term.reshape(8, 48, WIDTH),
            down_term.reshape(8, 72, WIDTH),
            jnp.zeros((8, 8, WIDTH), F32),
        ],
        axis=1,
    ).astype(BF)
    for step in range(4):
        for side in range(2):
            z_outs[step][side] = in_terms[side * 4 + lax.rem(z + step, 4)]
        quarter = lax.rem(y + step, 4)
        y_outs[step][...] = end_terms[:, pl.ds(pl.multiple_of(quarter * 32, 32), 32), :]


def qkv_term_kernel(where_ref, qkv_ref, qkv_kept_ref, qkv_arrived_ref, own_ref, sent_ref, terms):
    x_high = where_ref[0]
    for part in range(3):
        columns = slice(part * WIDTH, (part + 1) * WIDTH)
        term = both_terms(
            qkv_kept_ref[...],
            qkv_ref[:, columns],
            qkv_arrived_ref[:, 3 * WIDTH :],
            qkv_arrived_ref[:, columns],
        )
        terms[:, part * 48 : (part + 1) * 48, :] = term.reshape(8, 48, WIDTH).astype(BF)
    for out, side in ((own_ref, x_high), (sent_ref, 1 - x_high)):
        for block in range(4):
            out[block] = terms[side * 4 + block]


def attention_backward_kernel(
    where_ref, query_ref, key_ref, value_ref, grad_context_ref, row_ref, column_ref, log_ref,
    cosine_ref, sine_ref, normed_ref,
    handed_ref, kept_ref, rim_ref,
    key_sum, value_sum,
):
    core = where_ref[2]
    handed_ref[0:64, 0:WIDTH] = jnp.zeros((64, WIDTH), BF)
    handed_ref[320:384, 0:WIDTH] = jnp.zeros((64, WIDTH), BF)
    for block in range(2):
        rows = slice(block * 128, (block + 1) * 128)
        span = slice(block * 128, block * 128 + 256)
        bias = score_bias(row_ref, column_ref, block)
        for pair in range(6):
            cut = slice(pair * 128, (pair + 1) * 128)
            queries = both_heads(query_ref[rows, cut])
            grads = both_heads(grad_context_ref[rows, cut])
            keys = key_ref[span, cut]
            scores = matmul_turned(queries, keys) * score_scale + bias
            index = block * 6 + pair
            probs = jnp.exp(scores - log_ref[:, index : index + 1])
            grad_probs = matmul_turned(grads, value_ref[span, cut])
            inner = jnp.sum(probs * grad_probs, axis=-1, keepdims=True)
            grad_scores = (probs * (grad_probs - inner)).astype(BF)
            own = joined_heads(matmul(grad_scores, keys)) * score_scale
            turned = slice(64 + block * 128, 64 + (block + 1) * 128)
            handed_ref[turned, cut] = rotate_back(
                own, cosine_ref[turned, :], sine_ref[turned, :]
            ).astype(BF)
            key_part = turned_matmul(grad_scores, queries) * score_scale
            value_part = turned_matmul(probs.astype(BF), grads)
            if block == 0:
                key_sum[0:256, cut] = key_part
                value_sum[0:256, cut] = value_part
            else:
                key_sum[128:256, cut] += key_part[:128]
                value_sum[128:256, cut] += value_part[:128]
                key_sum[256:384, cut] = key_part[128:]
                value_sum[256:384, cut] = value_part[128:]
    for pair in range(6):
        cut = slice(pair * 128, (pair + 1) * 128)
        handed_ref[:, WIDTH + pair * 128 : WIDTH + (pair + 1) * 128] = rotate_back(
            key_sum[:, cut], cosine_ref[...], sine_ref[...]
        ).astype(BF)
    handed_ref[:, 2 * WIDTH : 3 * WIDTH] = value_sum[...].astype(BF)
    handed_ref[:, 3 * WIDTH :] = chosen(normed_ref[...], 1 - core, 48)
    kept_ref[...] = chosen(normed_ref[...], core, 48)
    rim_ref[...] = jnp.where(
        core == 0, handed_ref[0:64, WIDTH : 3 * WIDTH], handed_ref[320:384, WIDTH : 3 * WIDTH]
    )


def token_grad_kernel(
    where_ref, tokens_ref, grads_ref, other_ref, rim_ref,
    weight_ref, gain_ref, grad_hidden_ref, grad_tokens_ref,
):
    core = where_ref[2]
    total = matmul_turned(grads_ref[64:320, :WIDTH], weight_ref[:, :WIDTH])
    for part in (1, 2):
        cut = slice((part - 1) * WIDTH, part * WIDTH)
        own = slice(part * WIDTH, (part + 1) * WIDTH)
        far = rim_ref[:, cut].astype(F32)
        above = jnp.where(core == 0, far, other_ref[320:384, own].astype(F32))
        below = jnp.where(core == 0, other_ref[0:64, own].astype(F32), far)
        head = grads_ref[64:128, own].astype(F32) + above
        tail = grads_ref[256:320, own].astype(F32) + below
        rows = jnp.concatenate([head.astype(BF), grads_ref[128:256, own], tail.astype(BF)], axis=0)
        total = total + matmul_turned(rows, weight_ref[:, part * WIDTH : (part + 1) * WIDTH])
    standardized, inverse_scale = normalize_rows(tokens_ref[...].astype(F32))
    grad_tokens_ref[...] = (
        grad_hidden_ref[...]
        + norm_backward_pass(total * gain_ref[0:1, :], standardized, inverse_scale)
    ).astype(BF)


def call(kernel, arrays, outs, scratch=(), where=None, read=(), after=(), far=(), flops=0, vmem=12):
    first = [] if where is None else [pl.BlockSpec(memory_space=pltpu.SMEM)]
    in_vmem = pl.BlockSpec(memory_space=pltpu.VMEM)
    begin = len(first) + len(arrays) + len(read)

    def body(*refs):
        kernel(*refs[:begin], *refs[begin + len(after) :])

    return pl.pallas_call(
        body,
        out_shape=[jax.ShapeDtypeStruct(shape, kind) for shape, kind in outs],
        in_specs=first
        + [in_vmem] * len(arrays)
        + [pl.BlockSpec(memory_space=pltpu.HBM)] * len(read)
        + [pl.BlockSpec(memory_space=pl.ANY)] * len(after),
        out_specs=[
            pl.BlockSpec(memory_space=pltpu.HBM) if index in far else in_vmem
            for index in range(len(outs))
        ],
        scratch_shapes=[
            pltpu.VMEM(shape, kind) if kind else pltpu.SemaphoreType.DMA(shape)
            for shape, kind in scratch
        ],
        compiler_params=pltpu.CompilerParams(vmem_limit_bytes=vmem * 1024 * 1024),
        cost_estimate=pl.CostEstimate(flops=flops, bytes_accessed=0, transcendentals=0),
    )(*([] if where is None else [where]), *arrays, *read, *after)


def sum_of(refs, *index):
    total = refs[0][index].astype(F32)
    for ref in refs[1:]:
        total = total + ref[index].astype(F32)
    return total


def second_kernel(where_ref, *refs):
    z_refs, x_refs, y_refs, outs = refs[:4], refs[4:6], refs[6:10], refs[10:]
    x_high, z = where_ref[0], where_ref[1]
    for out, side in zip(outs[:2], (x_high, 1 - x_high)):
        out[0:144, :] = sum_of(z_refs, side).astype(BF)
        for block in range(4):
            rows = slice(144 + block * 32, 144 + (block + 1) * 32)
            out[rows, :] = sum_of(y_refs, side * 4 + block).astype(BF)
    for step in range(4):
        outs[2 + step][...] = sum_of(x_refs, lax.rem(z + step, 4)).astype(BF)


def third_kernel(where_ref, *refs):
    x_refs, z_refs, y_outs, z_outs, blocks, ends = refs[:2], refs[2:6], refs[6:10], refs[10:14], refs[14], refs[15]
    z, y = where_ref[1], where_ref[3]
    blocks[0:144, :] = sum_of(x_refs, slice(0, 144))
    blocks[144:288, :] = sum_of(z_refs)
    ends[...] = sum_of(x_refs, slice(144, 272)).reshape(4, 32, WIDTH)
    for step in range(4):
        rows = pl.ds(pl.multiple_of(lax.rem(y + step, 4) * 72, 8), 72)
        y_outs[step][...] = blocks[rows, :].astype(BF)
        z_outs[step][...] = ends[lax.rem(z + step, 4)].astype(BF)


def fourth_kernel(*refs):
    refs[8][...] = jnp.concatenate([sum_of(refs[:4]), sum_of(refs[4:8])], axis=0).astype(BF)


def twin_sum_kernel(*refs):
    refs[2][...] = sum_of(refs[:2]).astype(BF)


def final_weight(total, weight_ref, gain_ref, grad_ref, gain_grad_ref):
    dots = jnp.zeros((48, 128), F32)
    for part in range(3):
        cut = slice(part * WIDTH, (part + 1) * WIDTH)
        grad = total[part * 48 : (part + 1) * 48, :]
        grad_ref[:, cut] = grad
        products = weight_ref[:, cut].astype(F32) * grad
        for start in range(0, WIDTH, 128):
            dots = dots + products[:, start : start + 128]
    gain_grad_ref[...] = jnp.sum(dots.T, axis=0, keepdims=True) / gain_ref[...].astype(F32)


def final_kernel(
    where_ref, a, b, c, d, w_qkv_ref, gain1_ref, w_in_ref, gain2_ref,
    qkv_ref, qkv_gain_ref, in_ref, in_gain_ref, out_ref, down_ref, blocks, ends,
):
    y = where_ref[3]
    for step, part in enumerate((a, b, c, d)):
        quarter = lax.rem(y + step, 4)
        values = part[...].astype(F32)
        blocks[pl.ds(pl.multiple_of(quarter * 72, 8), 72), :] = values[:72]
        ends[pl.ds(pl.multiple_of(quarter * 32, 8), 32), :] = values[72:]
    final_weight(blocks[0:144, :], w_in_ref, gain2_ref, in_ref, in_gain_ref)
    final_weight(blocks[144:288, :], w_qkv_ref, gain1_ref, qkv_ref, qkv_gain_ref)
    out_ref[...] = ends[0:48, :]
    down_ref[...] = ends[48:120, :]


STEPS = (1, 2, 3)


def angles(position):
    fractions = jnp.arange(0, HEAD, 2).astype(F32) / HEAD
    inverse = jnp.exp(-math.log(10000.0) * fractions)
    phases = position.astype(F32)[:, None] * inverse[None, :]
    cosine, sine = jnp.cos(phases), jnp.sin(phases)
    return (
        jnp.concatenate([cosine] * 4, axis=1),
        jnp.concatenate([-sine, sine, -sine, sine], axis=1),
    )


def neighbours(count, step):
    return [(i, i + step) for i in range(count) if 0 <= i + step < count]


def shards(
    tokens, segment_ids, norm1_gain, w_qkv, w_attn_out, norm2_gain, w_in, w_mlp_out, cotangent
):
    row_count = tokens.shape[0]
    key_span = row_count + 2 * HALF
    at = place()
    where = jnp.stack([at["x_high"], at["z"], at["core"], at["y"]]).astype(jnp.int32)
    shard_place = at["shard"]

    (piece,) = call(
        pack_kernel,
        [],
        [((PACKED, WIDTH), BF)],
        scratch=[((1, 48), BF), ((1, 48), BF), ((72, WIDTH), BF), ((10,), None)],
        read=[w_qkv, norm1_gain[None, :], norm2_gain[None, :], w_attn_out, w_in, w_mlp_out],
        vmem=60,
    )
    own = {(0, 0): piece}
    own[1, 0] = send(piece, ACROSS_X)
    own[0, 3] = send(piece, Z_STEP[1])
    own[0, 1] = send(piece, Z_STEP[3])
    own[1, 1] = send(own[0, 1], ACROSS_X)
    own[1, 3] = send(own[1, 0], Z_STEP[1])
    own[0, 2] = send(own[0, 1], Z_STEP[3])
    tokens_above = lax.ppermute(tokens[row_count - HALF :], "shard", neighbours(16, 1))
    tokens_below = lax.ppermute(tokens[:HALF], "shard", neighbours(16, -1))

    first_row = shard_place * row_count
    seq_segs = segment_ids[0]
    segs_pad = jnp.pad(seq_segs, (HALF, HALF), constant_values=-1)
    key_segs = lax.dynamic_slice_in_dim(segs_pad, first_row, key_span, 0)
    own_segs = key_segs[HALF : HALF + row_count]
    earlier = jnp.sum((seq_segs[None, :] < key_segs[:, None]).astype(jnp.int32), axis=1)
    position = jnp.arange(key_span, dtype=jnp.int32) - HALF + first_row - earlier
    cosine_table, signed_sine = angles(position)
    row_segs, column_segs = own_segs[:, None], key_segs[None, :]

    square = (row_count, WIDTH)
    wide = (key_span, WIDTH)
    stacked, *thirds = call(
        stack_kernel,
        [own[key] for key in ((0, 0), (1, 0), (0, 3), (0, 1), (0, 2), (1, 3), (1, 1))],
        [((7, PACKED, WIDTH), BF)] + [((THIRD, WIDTH), BF)] * 3,
        after=[tokens_above, tokens_below, cosine_table, signed_sine, row_segs, column_segs, where],
    )
    pieces = [stacked] + [
        send(part, route) for part, route in zip(thirds, (ACROSS_X, Z_STEP[1], Z_STEP[3]))
    ]
    pieces += [send(value, OTHER_CORE) for value in pieces]
    (
        queries, keys, values, first_normed, wqkv_all, gain_table, log_total,
        output, grad_hidden, grad_context, mlp_handed, mlp_kept,
    ) = call(
        forward_kernel,
        [tokens, tokens_above, tokens_below, cotangent, cosine_table, signed_sine]
        + [row_segs, column_segs, *pieces],
        [(square, BF), (wide, BF), (wide, BF), (wide, BF), ((WIDTH, 3 * WIDTH), BF)]
        + [((16, WIDTH), F32), ((256, 128), F32)]
        + [(square, BF), (square, F32), (square, BF), ((256, HANDED), BF), ((256, 1344), BF)],
        scratch=[
            (square, BF),
            ((WIDTH, 3 * WIDTH), BF),
            ((16, WIDTH), F32),
            (square, F32),
            ((WIDTH, WIDTH), BF),
            ((WIDTH, 3 * WIDTH), BF),
            ((1152, WIDTH), BF),
            ((row_count, 1152), BF),
            ((3,), None),
        ],
        where=where,
        far=(4, 5, 8),
        vmem=24,
    )
    mlp_arrived = send(mlp_handed, OTHER_CORE)
    qkv_handed, qkv_kept, rim = call(
        attention_backward_kernel,
        [queries, keys, values, grad_context, row_segs, column_segs, log_total]
        + [cosine_table, signed_sine, first_normed],
        [((key_span, 3 * WIDTH + 384), BF), ((key_span, 384), BF)] + [((HALF, 2 * WIDTH), BF)],
        scratch=[(wide, F32), (wide, F32)],
        where=where,
    )
    qkv_arrived = send(qkv_handed, OTHER_CORE)
    rim_arrived = lax.ppermute(
        rim, "shard", [(i, i + 1) for i in range(1, 15, 2)] + [(i + 1, i) for i in range(1, 15, 2)]
    )
    stage = call(
        mlp_term_kernel,
        [mlp_handed, mlp_kept, mlp_arrived],
        [((2, 144, WIDTH), BF)] * 4 + [((8, 32, WIDTH), BF)] * 4,
        scratch=[((8, 144, WIDTH), BF), ((8, 128, WIDTH), BF)],
        where=where,
        after=[qkv_handed],
        flops=40_000_000_000,
    )
    z_parts, y_parts = stage[:4], stage[4:]
    x_parts = call(
        qkv_term_kernel,
        [qkv_handed, qkv_kept, qkv_arrived],
        [((4, 144, WIDTH), BF)] * 2,
        scratch=[((8, 144, WIDTH), BF)],
        where=where,
        after=[z_parts[0], rim_arrived],
        flops=40_000_000_000,
    )
    x_arrived = send(x_parts[1], ACROSS_X)
    z_arrived = [send(z_parts[step], Z_STEP[step]) for step in (1, 3)]
    z_arrived.append(send(hold(z_parts[2], z_arrived[0]), Z_STEP[2]))
    y_arrived = [send(y_parts[step], Y_STEP[step]) for step in (1, 3)]
    y_arrived.append(send(hold(y_parts[2], y_arrived[0]), Y_STEP[2]))
    (grad_tokens,) = call(
        token_grad_kernel,
        [tokens, qkv_handed, qkv_arrived, rim_arrived, wqkv_all, gain_table, grad_hidden],
        [(square, BF)],
        where=where,
        after=[x_parts[0]],
        flops=40_000_000_000,
    )
    stage = call(
        second_kernel,
        [z_parts[0], *z_arrived, x_parts[0], x_arrived, y_parts[0], *y_arrived],
        [((272, WIDTH), BF)] * 2 + [((144, WIDTH), BF)] * 4,
        where=where,
        after=[grad_tokens],
    )
    x_arrived = send(stage[1], ACROSS_X)
    z_arrived = [send(stage[2 + step], Z_STEP[step]) for step in STEPS]
    stage = call(
        third_kernel,
        [stage[0], x_arrived, stage[2], *z_arrived],
        [((72, WIDTH), BF)] * 4 + [((32, WIDTH), BF)] * 4,
        scratch=[((288, WIDTH), F32), ((4, 32, WIDTH), F32)],
        where=where,
    )
    y_arrived = [send(stage[step], Y_STEP[step]) for step in STEPS]
    z_arrived = [send(stage[4 + step], Z_STEP[step]) for step in STEPS]
    part = [((104, WIDTH), BF)]
    (total,) = call(fourth_kernel, [stage[0], *y_arrived, stage[4], *z_arrived], part)
    (total,) = call(twin_sum_kernel, [total, send(total, TWIN_X)], part)
    quarters = [total] + [send(total, Y_STEP[4 - step]) for step in STEPS]
    columns = (48, 3 * WIDTH)
    grad_w_qkv, gain1, grad_w_in, gain2, grad_w_out, grad_w_down = call(
        final_kernel,
        [*quarters, w_qkv, norm1_gain[None, :], w_in, norm2_gain[None, :]],
        [(columns, F32), ((1, 48), F32), (columns, F32), ((1, 48), F32)]
        + [((48, WIDTH), F32), ((72, WIDTH), F32)],
        scratch=[((288, WIDTH), F32), ((128, WIDTH), F32)],
        where=where,
    )
    return (
        output, grad_tokens, gain1[0], grad_w_qkv, grad_w_out, gain2[0], grad_w_in, grad_w_down
    )


def solution(mesh):
    return jax.shard_map(
        shards,
        mesh=mesh,
        in_specs=(
            P(("rep", "shard"), None),
            P("rep", None),
            P("shard"),
            P("shard", None),
            P("shard", None),
            P("shard"),
            P("shard", None),
            P("shard", None),
            P(("rep", "shard"), None),
        ),
        out_specs=(
            P(("rep", "shard"), None),
            P(("rep", "shard"), None),
            P("shard"),
            P("shard", None),
            P("shard", None),
            P("shard"),
            P("shard", None),
            P("shard", None),
        ),
        check_vma=False,
    )
```

```python
import functools
import math

import jax
import jax.numpy as jnp
from jax import lax
from jax.experimental import pallas as pl
from jax.experimental.pallas import tpu as pltpu
from jax.sharding import PartitionSpec as P

HEADS = 12
HEAD = 64
HALF = 64
WIDTH = 768
AXES = ("rep", "shard")
BF = jnp.bfloat16
F32 = jnp.float32

norm_epsilon = 1e-05
masked_score = -1e30
root_half = 0.7071067811865476
density_factor = 0.3989422804014327
score_scale = 0.125


def coordinates(device):
    rep, shard = divmod(device, 16)
    x_low, y = divmod(rep, 4)
    x_high, rest = divmod(shard, 8)
    z, core = divmod(rest, 2)
    return x_high * 2 + x_low, y, z, core


def number(x, y, z, core):
    return ((x % 2) * 4 + y) * 16 + (x // 2) * 8 + z * 2 + core


def pairs(move):
    return [(device, number(*move(*coordinates(device)))) for device in range(128)]


def along_z(step):
    return pairs(lambda x, y, z, core: (x, y, (z + step) % 4, core))


def along_y(step):
    return pairs(lambda x, y, z, core: (x, (y + step) % 4, z, core))


OTHER_CORE = pairs(lambda x, y, z, core: (x, y, z, 1 - core))
ACROSS_X = pairs(lambda x, y, z, core: (3 - x, y, z, core))
TWIN_X = pairs(lambda x, y, z, core: (x ^ 1, y, z, core))
Z_STEP = {step: along_z(step) for step in (1, 2, 3)}
Y_STEP = {step: along_y(step) for step in (1, 2, 3)}


def send(value, route):
    return lax.ppermute(value, AXES, route)


def place():
    shard = lax.axis_index("shard")
    rep = lax.axis_index("rep")
    return {
        "x_high": shard // 8,
        "z": (shard // 2) % 4,
        "core": shard % 2,
        "x_low": rep // 4,
        "y": rep % 4,
        "shard": shard,
    }


PIECES = [(0, 0), (1, 0), (0, 3), (0, 1), (0, 2), (1, 3), (1, 1), (1, 2)]
THIRD = 144


def stack_kernel(*refs):
    pieces, stacked_ref, thirds = refs[:7], refs[7], refs[8:]
    for index, piece in enumerate(pieces):
        stacked_ref[index] = piece[...]
    for index, third in enumerate(thirds):
        third[...] = pieces[4 + index][index * THIRD : (index + 1) * THIRD, :]


def hold_kernel(value_ref, earlier_ref, held_ref):
    pass


def hold(value, earlier):
    return pl.pallas_call(
        hold_kernel,
        out_shape=jax.ShapeDtypeStruct(value.shape, value.dtype),
        in_specs=[pl.BlockSpec(memory_space=pl.ANY)] * 2,
        out_specs=pl.BlockSpec(memory_space=pl.ANY),
        input_output_aliases={0: 0},
    )(value, earlier)


GAINS = slice(144, 160)
OUT = 160
IN = 208
DOWN = 352
PACKED = 432


def pack_kernel(
    qkv_ref, gain1_ref, gain2_ref, out_ref, in_ref, down_ref, piece_ref, gain1, gain2, down, done
):
    moves = [(gain1_ref, gain1), (gain2_ref, gain2), (down_ref, down)]
    moves.append((out_ref, piece_ref.at[pl.ds(OUT, 48), :]))
    for part in range(3):
        cut = pl.ds(part * WIDTH, WIDTH)
        moves.append((qkv_ref.at[:, cut], piece_ref.at[pl.ds(part * 48, 48), :]))
        moves.append((in_ref.at[:, cut], piece_ref.at[pl.ds(IN + part * 48, 48), :]))
    copies = [
        pltpu.make_async_copy(source, target, done.at[index])
        for index, (source, target) in enumerate(moves)
    ]
    for copy in copies:
        copy.start()
    first = lax.axis_index("shard") * 48
    row = lax.broadcasted_iota(jnp.int32, (48, WIDTH), 0)
    own_lanes = jnp.where(lanes_of((48, WIDTH)) == row + first, 1.0, 0.0).astype(BF)
    which = lax.broadcasted_iota(jnp.int32, (16, 48), 0)
    for copy in copies[:3]:
        copy.wait()
    gains = jnp.where(
        which == 0,
        gain1[...].astype(F32),
        jnp.where(which == 1, gain2[...].astype(F32), 0.0),
    )
    piece_ref[GAINS, :] = matmul(gains.astype(BF), own_lanes).astype(BF)
    padded = jnp.concatenate([down[...].astype(F32), jnp.zeros((8, WIDTH), F32)], axis=0)
    piece_ref[DOWN:, :] = padded.astype(BF)
    for copy in copies[3:]:
        copy.wait()


def chip_blocks(where_ref):
    x_high, z = where_ref[0], where_ref[1]
    sides = [1 - x_high if turned else x_high for turned, _ in PIECES]
    return [side * 4 + lax.rem(z + step, 4) for side, (_, step) in zip(sides, PIECES)]


def at_rows(block, count):
    return pl.ds(pl.multiple_of(block * count, 16), count)


def packed_rows(pieces, index, first, last):
    core, number_of = divmod(index, 8)
    stacked, *thirds = pieces[4 * core : 4 * core + 4]
    if number_of < 7:
        return stacked[number_of, first:last, :]
    found = []
    for position, third in enumerate(thirds):
        begin, end = max(first - position * THIRD, 0), min(last - position * THIRD, THIRD)
        if begin < end:
            found.append(third[begin:end, :])
    return found[0] if len(found) == 1 else jnp.concatenate(found, axis=0)


def place_rows(where_ref, pieces, weight_ref, start, parts):
    core = where_ref[2]
    for index, chip in enumerate(chip_blocks(where_ref)):
        for source, block in ((index, 2 * chip + core), (8 + index, 2 * chip + 1 - core)):
            for part in range(parts):
                columns = slice(part * WIDTH, (part + 1) * WIDTH)
                weight_ref[at_rows(block, 48), columns] = packed_rows(
                    pieces, source, start + part * 48, start + (part + 1) * 48
                )


def chosen_columns(core, rows, count):
    row = lax.broadcasted_iota(jnp.int32, (rows, rows // 2), 0)
    column = lax.broadcasted_iota(jnp.int32, (rows, rows // 2), 1)
    wanted = (column // count * 2 + core) * count + lax.rem(column, count)
    return jnp.where(row == wanted, 1.0, 0.0).astype(BF)


def chosen(values, core, count):
    picked = matmul(values, chosen_columns(core, values.shape[1], count))
    return picked.astype(BF)


def matmul(a, b):
    return jnp.dot(a, b, preferred_element_type=F32)


def matmul_turned(a, b):
    return lax.dot_general(a, b, (((1,), (1,)), ((), ())), preferred_element_type=F32)


def turned_matmul(a, b):
    return lax.dot_general(a, b, (((0,), (0,)), ((), ())), preferred_element_type=F32)


def normalize_rows(values):
    centre = values - jnp.mean(values, axis=-1, keepdims=True)
    spread = jnp.mean(centre * centre, axis=-1, keepdims=True)
    row_inverse_scale = lax.rsqrt(spread + norm_epsilon)
    return (centre * row_inverse_scale, row_inverse_scale)


def norm_backward_pass(normalized_gradient, standardized_rows, row_inverse_scale):
    centered_average = jnp.mean(normalized_gradient, axis=-1, keepdims=True)
    projected_average = jnp.mean(normalized_gradient * standardized_rows, axis=-1, keepdims=True)
    return row_inverse_scale * (
        normalized_gradient - centered_average - standardized_rows * projected_average
    )


def lanes_of(shape):
    return lax.broadcasted_iota(jnp.int32, shape, 1)


def turn_halves(values):
    low = lax.rem(lanes_of(values.shape), 64) < 32
    return jnp.where(low, pltpu.roll(values, 96, 1), pltpu.roll(values, 32, 1))


def rotate(vectors, cosine_table, signed_sine):
    return vectors * cosine_table + turn_halves(vectors) * signed_sine


def rotate_back(vectors, cosine_table, signed_sine):
    return vectors * cosine_table + turn_halves(vectors * signed_sine)


def qkv_part(
    where_ref, tokens_ref, above_ref, below_ref, cosine_ref, sine_ref, pieces,
    query_ref, key_ref, value_ref, normed_ref, weight_ref, gain_ref,
):
    place_rows(where_ref, pieces, weight_ref, 0, 3)
    gains = jnp.zeros((16, WIDTH), F32)
    for index in range(16):
        gains = gains + packed_rows(pieces, index, GAINS.start, GAINS.stop).astype(F32)
    gain_ref[...] = gains
    for source, rows in ((above_ref, slice(0, 64)), (tokens_ref, slice(64, 320)), (below_ref, slice(320, 384))):
        standardized, _ = normalize_rows(source[...].astype(F32))
        normed_ref[rows, :] = (standardized * gains[0:1, :]).astype(BF)
    for wide in range(0, WIDTH, 256):
        query = matmul(normed_ref[64:320, :], weight_ref[:, wide : wide + 256])
        key = matmul(normed_ref[...], weight_ref[:, WIDTH + wide : WIDTH + wide + 256])
        for half in range(0, 256, 128):
            cut, here = slice(wide + half, wide + half + 128), slice(half, half + 128)
            query_ref[:, cut] = rotate(
                query[:, here], cosine_ref[64:320, :], sine_ref[64:320, :]
            ).astype(BF)
            key_ref[:, cut] = rotate(key[:, here], cosine_ref[...], sine_ref[...]).astype(BF)
    value_ref[...] = matmul(normed_ref[...], weight_ref[:, 2 * WIDTH :]).astype(BF)


def score_bias(row_segments_ref, column_segments_ref, block):
    rows = slice(block * 128, (block + 1) * 128)
    columns = slice(block * 128, block * 128 + 256)
    row = lax.broadcasted_iota(jnp.int32, (128, 256), 0)
    column = lanes_of((128, 256))
    allowed = (
        (column >= row)
        & (column <= row + 2 * HALF)
        & (row_segments_ref[rows, :] == column_segments_ref[:, columns])
    )
    bias = jnp.where(allowed, 0.0, masked_score)
    return jnp.concatenate([bias, bias], axis=0)


def both_heads(values):
    first = lanes_of(values.shape) < 64
    empty = jnp.zeros_like(values)
    return jnp.concatenate([jnp.where(first, values, empty), jnp.where(first, empty, values)], axis=0)


def joined_heads(values):
    return jnp.where(lanes_of((128, 128)) < 64, values[:128], values[128:])


def attention_part(query_ref, key_ref, value_ref, row_ref, column_ref, context_ref, log_ref):
    logs = jnp.zeros((256, 128), F32)
    lane = lanes_of((256, 128))
    for block in range(2):
        rows = slice(block * 128, (block + 1) * 128)
        span = slice(block * 128, block * 128 + 256)
        bias = score_bias(row_ref, column_ref, block)
        for pair in range(6):
            cut = slice(pair * 128, (pair + 1) * 128)
            queries = both_heads(query_ref[rows, cut])
            scores = matmul_turned(queries, key_ref[span, cut]) * score_scale + bias
            top = jnp.max(scores, axis=-1, keepdims=True)
            exponent = jnp.exp(scores - top)
            total = jnp.sum(exponent, axis=-1, keepdims=True)
            probs = (exponent * (1.0 / total)).astype(BF)
            context_ref[rows, cut] = joined_heads(matmul(probs, value_ref[span, cut])).astype(BF)
            logs = jnp.where(lane == block * 6 + pair, top + jnp.log(total), logs)
    log_ref[...] = logs


GATE_UP = slice(0, 2304)
COTANGENT = slice(2304, 3072)
GRAD_ATTN = slice(3072, 3840)
NORMED = slice(3840, 4224)
CONTEXT = slice(4224, 4608)
MIXED = slice(4608, 5184)
HANDED = 5248


CHUNK = 1152


def mlp_part(
    where_ref, tokens_ref, context_ref, cotangent_ref, gain_ref, pieces,
    output_ref, grad_hidden_ref, grad_context_ref, handed_ref, kept_ref,
    out_weight, in_weight, down_weight, mixed_rows, hidden_done,
):
    core = where_ref[2]
    place_rows(where_ref, pieces, out_weight, OUT, 1)
    place_rows(where_ref, pieces, in_weight, IN, 3)
    for index, chip in enumerate(chip_blocks(where_ref)):
        here = packed_rows(pieces, index, DOWN, PACKED).astype(F32)[:72]
        there = packed_rows(pieces, 8 + index, DOWN, PACKED).astype(F32)[:72]
        first = jnp.where(core == 0, here, there)
        second = jnp.where(core == 0, there, here)
        down_weight[at_rows(chip, 144), :] = jnp.concatenate([first, second], axis=0).astype(BF)

    gain = gain_ref[1:2, :]
    hidden = tokens_ref[...].astype(F32) + matmul(context_ref[...], out_weight[...])
    standardized, inverse_scale = normalize_rows(hidden)
    normed = (standardized * gain).astype(BF)
    cotangent = cotangent_ref[...]
    total = hidden
    for chunk in range(1152 // CHUNK):
        cut = slice(chunk * CHUNK, (chunk + 1) * CHUNK)
        second_cut = slice(1152 + chunk * CHUNK, 1152 + (chunk + 1) * CHUNK)
        gate = matmul(normed, in_weight[:, cut])
        up = matmul(normed, in_weight[:, second_cut])
        normal_cdf = 0.5 * (1.0 + lax.erf(gate * root_half))
        normal_pdf = jnp.exp(-0.5 * gate * gate) * density_factor
        activated = gate * normal_cdf
        mixed = (activated * up).astype(BF)
        mixed_rows[:, cut] = mixed
        total = total + matmul(mixed, down_weight[cut, :])
        grad_mixed = matmul_turned(cotangent, down_weight[cut, :])
        handed_ref[:, cut] = (grad_mixed * up * (normal_cdf + gate * normal_pdf)).astype(BF)
        handed_ref[:, second_cut] = (grad_mixed * activated).astype(BF)
    output_ref[...] = total.astype(BF)

    grad_normed = matmul_turned(handed_ref[:, GATE_UP], in_weight[...])
    grad_hidden = cotangent.astype(F32) + norm_backward_pass(
        grad_normed * gain, standardized, inverse_scale
    )
    grad_hidden_ref[...] = grad_hidden
    hidden_done()
    grad_attn = grad_hidden.astype(BF)
    grad_context_ref[...] = matmul_turned(grad_attn, out_weight[...]).astype(BF)
    handed_ref[:, COTANGENT] = cotangent
    handed_ref[:, GRAD_ATTN] = grad_attn
    handed_ref[:, 5120:] = jnp.zeros((256, 128), BF)
    for target, owner, offset in ((kept_ref, core, 0), (handed_ref, 1 - core, NORMED.start)):
        target[:, offset : offset + 384] = chosen(normed, owner, 48)
        target[:, offset + 384 : offset + 768] = chosen(context_ref[...], owner, 48)
        target[:, offset + 768 : offset + 1344] = chosen(mixed_rows[...], owner, 72)


def forward_kernel(
    where_ref, tokens_ref, above_ref, below_ref, cotangent_ref, cosine_ref, sine_ref,
    row_ref, column_ref, *refs
):
    pieces, rest = refs[:8], refs[8:]
    (
    query_ref, key_ref, value_ref, normed_ref, far_weight_ref, far_gain_ref, log_ref,
    output_ref, far_hidden_ref, grad_context_ref, handed_ref, kept_ref,
    context, weight, gain_ref, grad_hidden_ref, out_weight, in_weight, down_weight, mixed_rows,
    written,
    ) = rest
    qkv_part(
        where_ref, tokens_ref, above_ref, below_ref, cosine_ref, sine_ref, pieces,
        query_ref, key_ref, value_ref, normed_ref, weight, gain_ref,
    )
    copies = [
        pltpu.make_async_copy(source, target, written.at[index])
        for index, (source, target) in enumerate(
            ((weight, far_weight_ref), (gain_ref, far_gain_ref), (grad_hidden_ref, far_hidden_ref))
        )
    ]
    copies[0].start()
    copies[1].start()
    attention_part(query_ref, key_ref, value_ref, row_ref, column_ref, context, log_ref)
    mlp_part(
        where_ref, tokens_ref, context, cotangent_ref, gain_ref, pieces,
        output_ref, grad_hidden_ref, grad_context_ref, handed_ref, kept_ref,
        out_weight, in_weight, down_weight, mixed_rows, copies[2].start,
    )
    for copy in copies:
        copy.wait()


def both_terms(own_left, own_right, arrived_left, arrived_right):
    return turned_matmul(own_left, own_right) + turned_matmul(arrived_left, arrived_right)


def mlp_term_kernel(where_ref, mlp_ref, mlp_kept_ref, mlp_arrived_ref, *rest):
    z_outs, y_outs, (in_terms, end_terms) = rest[:4], rest[4:8], rest[8:]
    z, y = where_ref[1], where_ref[3]
    for part in range(3):
        columns = slice(part * WIDTH, (part + 1) * WIDTH)
        term = both_terms(
            mlp_kept_ref[:, 0:384],
            mlp_ref[:, columns],
            mlp_arrived_ref[:, NORMED],
            mlp_arrived_ref[:, columns],
        )
        in_terms[:, part * 48 : (part + 1) * 48, :] = term.reshape(8, 48, WIDTH).astype(BF)
    out_term = both_terms(
        mlp_kept_ref[:, 384:768],
        mlp_ref[:, GRAD_ATTN],
        mlp_arrived_ref[:, CONTEXT],
        mlp_arrived_ref[:, GRAD_ATTN],
    )
    down_term = both_terms(
        mlp_kept_ref[:, 768:1344],
        mlp_ref[:, COTANGENT],
        mlp_arrived_ref[:, MIXED],
        mlp_arrived_ref[:, COTANGENT],
    )
    end_terms[...] = jnp.concatenate(
        [
            out_term.reshape(8, 48, WIDTH),
            down_term.reshape(8, 72, WIDTH),
            jnp.zeros((8, 8, WIDTH), F32),
        ],
        axis=1,
    ).astype(BF)
    for step in range(4):
        for side in range(2):
            z_outs[step][side] = in_terms[side * 4 + lax.rem(z + step, 4)]
        quarter = lax.rem(y + step, 4)
        y_outs[step][...] = end_terms[:, pl.ds(pl.multiple_of(quarter * 32, 32), 32), :]


def qkv_term_kernel(where_ref, qkv_ref, qkv_kept_ref, qkv_arrived_ref, own_ref, sent_ref, terms):
    x_high = where_ref[0]
    for part in range(3):
        columns = slice(part * WIDTH, (part + 1) * WIDTH)
        term = both_terms(
            qkv_kept_ref[...],
            qkv_ref[:, columns],
            qkv_arrived_ref[:, 3 * WIDTH :],
            qkv_arrived_ref[:, columns],
        )
        terms[:, part * 48 : (part + 1) * 48, :] = term.reshape(8, 48, WIDTH).astype(BF)
    for out, side in ((own_ref, x_high), (sent_ref, 1 - x_high)):
        for block in range(4):
            out[block] = terms[side * 4 + block]


def attention_backward_kernel(
    where_ref, query_ref, key_ref, value_ref, grad_context_ref, row_ref, column_ref, log_ref,
    cosine_ref, sine_ref, normed_ref,
    handed_ref, kept_ref, rim_ref,
    key_sum, value_sum,
):
    core = where_ref[2]
    handed_ref[0:64, 0:WIDTH] = jnp.zeros((64, WIDTH), BF)
    handed_ref[320:384, 0:WIDTH] = jnp.zeros((64, WIDTH), BF)
    for block in range(2):
        rows = slice(block * 128, (block + 1) * 128)
        span = slice(block * 128, block * 128 + 256)
        bias = score_bias(row_ref, column_ref, block)
        for pair in range(6):
            cut = slice(pair * 128, (pair + 1) * 128)
            queries = both_heads(query_ref[rows, cut])
            grads = both_heads(grad_context_ref[rows, cut])
            keys = key_ref[span, cut]
            scores = matmul_turned(queries, keys) * score_scale + bias
            index = block * 6 + pair
            probs = jnp.exp(scores - log_ref[:, index : index + 1])
            grad_probs = matmul_turned(grads, value_ref[span, cut])
            inner = jnp.sum(probs * grad_probs, axis=-1, keepdims=True)
            grad_scores = (probs * (grad_probs - inner)).astype(BF)
            own = joined_heads(matmul(grad_scores, keys)) * score_scale
            turned = slice(64 + block * 128, 64 + (block + 1) * 128)
            handed_ref[turned, cut] = rotate_back(
                own, cosine_ref[turned, :], sine_ref[turned, :]
            ).astype(BF)
            key_part = turned_matmul(grad_scores, queries) * score_scale
            value_part = turned_matmul(probs.astype(BF), grads)
            if block == 0:
                key_sum[0:256, cut] = key_part
                value_sum[0:256, cut] = value_part
            else:
                key_sum[128:256, cut] += key_part[:128]
                value_sum[128:256, cut] += value_part[:128]
                key_sum[256:384, cut] = key_part[128:]
                value_sum[256:384, cut] = value_part[128:]
    for pair in range(6):
        cut = slice(pair * 128, (pair + 1) * 128)
        handed_ref[:, WIDTH + pair * 128 : WIDTH + (pair + 1) * 128] = rotate_back(
            key_sum[:, cut], cosine_ref[...], sine_ref[...]
        ).astype(BF)
    handed_ref[:, 2 * WIDTH : 3 * WIDTH] = value_sum[...].astype(BF)
    handed_ref[:, 3 * WIDTH :] = chosen(normed_ref[...], 1 - core, 48)
    kept_ref[...] = chosen(normed_ref[...], core, 48)
    rim_ref[...] = jnp.where(
        core == 0, handed_ref[0:64, WIDTH : 3 * WIDTH], handed_ref[320:384, WIDTH : 3 * WIDTH]
    )


def token_grad_kernel(
    where_ref, tokens_ref, grads_ref, other_ref, rim_ref,
    weight_ref, gain_ref, grad_hidden_ref, grad_tokens_ref,
):
    core = where_ref[2]
    total = matmul_turned(grads_ref[64:320, :WIDTH], weight_ref[:, :WIDTH])
    for part in (1, 2):
        cut = slice((part - 1) * WIDTH, part * WIDTH)
        own = slice(part * WIDTH, (part + 1) * WIDTH)
        far = rim_ref[:, cut].astype(F32)
        above = jnp.where(core == 0, far, other_ref[320:384, own].astype(F32))
        below = jnp.where(core == 0, other_ref[0:64, own].astype(F32), far)
        head = grads_ref[64:128, own].astype(F32) + above
        tail = grads_ref[256:320, own].astype(F32) + below
        rows = jnp.concatenate([head.astype(BF), grads_ref[128:256, own], tail.astype(BF)], axis=0)
        total = total + matmul_turned(rows, weight_ref[:, part * WIDTH : (part + 1) * WIDTH])
    standardized, inverse_scale = normalize_rows(tokens_ref[...].astype(F32))
    grad_tokens_ref[...] = (
        grad_hidden_ref[...]
        + norm_backward_pass(total * gain_ref[0:1, :], standardized, inverse_scale)
    ).astype(BF)


def call(kernel, arrays, outs, scratch=(), where=None, read=(), after=(), far=(), flops=0, vmem=12):
    first = [] if where is None else [pl.BlockSpec(memory_space=pltpu.SMEM)]
    in_vmem = pl.BlockSpec(memory_space=pltpu.VMEM)
    begin = len(first) + len(arrays) + len(read)

    def body(*refs):
        kernel(*refs[:begin], *refs[begin + len(after) :])

    return pl.pallas_call(
        body,
        out_shape=[jax.ShapeDtypeStruct(shape, kind) for shape, kind in outs],
        in_specs=first
        + [in_vmem] * len(arrays)
        + [pl.BlockSpec(memory_space=pltpu.HBM)] * len(read)
        + [pl.BlockSpec(memory_space=pl.ANY)] * len(after),
        out_specs=[
            pl.BlockSpec(memory_space=pltpu.HBM) if index in far else in_vmem
            for index in range(len(outs))
        ],
        scratch_shapes=[
            pltpu.VMEM(shape, kind) if kind else pltpu.SemaphoreType.DMA(shape)
            for shape, kind in scratch
        ],
        compiler_params=pltpu.CompilerParams(vmem_limit_bytes=vmem * 1024 * 1024),
        cost_estimate=pl.CostEstimate(flops=flops, bytes_accessed=0, transcendentals=0),
    )(*([] if where is None else [where]), *arrays, *read, *after)


def sum_of(refs, *index):
    total = refs[0][index].astype(F32)
    for ref in refs[1:]:
        total = total + ref[index].astype(F32)
    return total


def second_across_kernel(where_ref, *refs):
    z_refs, y_refs, outs = refs[:4], refs[4:8], refs[8:]
    x_high = where_ref[0]
    for out, side in zip(outs, (x_high, 1 - x_high)):
        out[0:144, :] = sum_of(z_refs, side).astype(BF)
        for block in range(4):
            rows = slice(144 + block * 32, 144 + (block + 1) * 32)
            out[rows, :] = sum_of(y_refs, side * 4 + block).astype(BF)


def second_along_kernel(where_ref, *refs):
    x_refs, outs = refs[:2], refs[2:]
    for step in range(4):
        outs[step][...] = sum_of(x_refs, lax.rem(where_ref[1] + step, 4)).astype(BF)


def third_along_kernel(where_ref, own_ref, arrived_ref, *rest):
    outs, ends = rest[:4], rest[4]
    ends[...] = sum_of((own_ref, arrived_ref), slice(144, 272)).reshape(4, 32, WIDTH)
    for step in range(4):
        outs[step][...] = ends[lax.rem(where_ref[1] + step, 4)].astype(BF)


def third_kernel(where_ref, *refs):
    x_refs, z_refs, outs, blocks = refs[:2], refs[2:6], refs[6:10], refs[10]
    blocks[0:144, :] = sum_of(x_refs, slice(0, 144))
    blocks[144:288, :] = sum_of(z_refs)
    for step in range(4):
        rows = pl.ds(pl.multiple_of(lax.rem(where_ref[3] + step, 4) * 72, 8), 72)
        outs[step][...] = blocks[rows, :].astype(BF)


def fourth_kernel(*refs):
    refs[8][...] = jnp.concatenate([sum_of(refs[:4]), sum_of(refs[4:8])], axis=0).astype(BF)


def twin_sum_kernel(*refs):
    refs[2][...] = sum_of(refs[:2]).astype(BF)


def final_weight(total, weight_ref, gain_ref, grad_ref, gain_grad_ref):
    dots = jnp.zeros((48, 128), F32)
    for part in range(3):
        cut = slice(part * WIDTH, (part + 1) * WIDTH)
        grad = total[part * 48 : (part + 1) * 48, :]
        grad_ref[:, cut] = grad
        products = weight_ref[:, cut].astype(F32) * grad
        for start in range(0, WIDTH, 128):
            dots = dots + products[:, start : start + 128]
    gain_grad_ref[...] = jnp.sum(dots.T, axis=0, keepdims=True) / gain_ref[...].astype(F32)


def final_kernel(
    where_ref, a, b, c, d, w_qkv_ref, gain1_ref, w_in_ref, gain2_ref,
    qkv_ref, qkv_gain_ref, in_ref, in_gain_ref, out_ref, down_ref, blocks, ends,
):
    y = where_ref[3]
    for step, part in enumerate((a, b, c, d)):
        quarter = lax.rem(y + step, 4)
        values = part[...].astype(F32)
        blocks[pl.ds(pl.multiple_of(quarter * 72, 8), 72), :] = values[:72]
        ends[pl.ds(pl.multiple_of(quarter * 32, 8), 32), :] = values[72:]
    final_weight(blocks[0:144, :], w_in_ref, gain2_ref, in_ref, in_gain_ref)
    final_weight(blocks[144:288, :], w_qkv_ref, gain1_ref, qkv_ref, qkv_gain_ref)
    out_ref[...] = ends[0:48, :]
    down_ref[...] = ends[48:120, :]


STEPS = (1, 2, 3)


def angles(position):
    fractions = jnp.arange(0, HEAD, 2).astype(F32) / HEAD
    inverse = jnp.exp(-math.log(10000.0) * fractions)
    phases = position.astype(F32)[:, None] * inverse[None, :]
    cosine, sine = jnp.cos(phases), jnp.sin(phases)
    return (
        jnp.concatenate([cosine] * 4, axis=1),
        jnp.concatenate([-sine, sine, -sine, sine], axis=1),
    )


def neighbours(count, step):
    return [(i, i + step) for i in range(count) if 0 <= i + step < count]


def shards(
    tokens, segment_ids, norm1_gain, w_qkv, w_attn_out, norm2_gain, w_in, w_mlp_out, cotangent
):
    row_count = tokens.shape[0]
    key_span = row_count + 2 * HALF
    at = place()
    where = jnp.stack([at["x_high"], at["z"], at["core"], at["y"]]).astype(jnp.int32)
    shard_place = at["shard"]

    (piece,) = call(
        pack_kernel,
        [],
        [((PACKED, WIDTH), BF)],
        scratch=[((1, 48), BF), ((1, 48), BF), ((72, WIDTH), BF), ((10,), None)],
        read=[w_qkv, norm1_gain[None, :], norm2_gain[None, :], w_attn_out, w_in, w_mlp_out],
        vmem=60,
    )
    own = {(0, 0): piece}
    own[1, 0] = send(piece, ACROSS_X)
    own[0, 3] = send(piece, Z_STEP[1])
    own[0, 1] = send(piece, Z_STEP[3])
    own[1, 1] = send(own[0, 1], ACROSS_X)
    own[1, 3] = send(own[1, 0], Z_STEP[1])
    own[0, 2] = send(own[0, 1], Z_STEP[3])
    tokens_above = lax.ppermute(tokens[row_count - HALF :], "shard", neighbours(16, 1))
    tokens_below = lax.ppermute(tokens[:HALF], "shard", neighbours(16, -1))

    first_row = shard_place * row_count
    seq_segs = segment_ids[0]
    segs_pad = jnp.pad(seq_segs, (HALF, HALF), constant_values=-1)
    key_segs = lax.dynamic_slice_in_dim(segs_pad, first_row, key_span, 0)
    own_segs = key_segs[HALF : HALF + row_count]
    earlier = jnp.sum((seq_segs[None, :] < key_segs[:, None]).astype(jnp.int32), axis=1)
    position = jnp.arange(key_span, dtype=jnp.int32) - HALF + first_row - earlier
    cosine_table, signed_sine = angles(position)
    row_segs, column_segs = own_segs[:, None], key_segs[None, :]

    square = (row_count, WIDTH)
    wide = (key_span, WIDTH)
    stacked, *thirds = call(
        stack_kernel,
        [own[key] for key in ((0, 0), (1, 0), (0, 3), (0, 1), (0, 2), (1, 3), (1, 1))],
        [((7, PACKED, WIDTH), BF)] + [((THIRD, WIDTH), BF)] * 3,
        after=[tokens_above, tokens_below, cosine_table, signed_sine, row_segs, column_segs, where],
    )
    pieces = [stacked] + [
        send(part, route) for part, route in zip(thirds, (ACROSS_X, Z_STEP[1], Z_STEP[3]))
    ]
    pieces += [send(value, OTHER_CORE) for value in pieces]
    (
        queries, keys, values, first_normed, wqkv_all, gain_table, log_total,
        output, grad_hidden, grad_context, mlp_handed, mlp_kept,
    ) = call(
        forward_kernel,
        [tokens, tokens_above, tokens_below, cotangent, cosine_table, signed_sine]
        + [row_segs, column_segs, *pieces],
        [(square, BF), (wide, BF), (wide, BF), (wide, BF), ((WIDTH, 3 * WIDTH), BF)]
        + [((16, WIDTH), F32), ((256, 128), F32)]
        + [(square, BF), (square, F32), (square, BF), ((256, HANDED), BF), ((256, 1344), BF)],
        scratch=[
            (square, BF),
            ((WIDTH, 3 * WIDTH), BF),
            ((16, WIDTH), F32),
            (square, F32),
            ((WIDTH, WIDTH), BF),
            ((WIDTH, 3 * WIDTH), BF),
            ((1152, WIDTH), BF),
            ((row_count, 1152), BF),
            ((3,), None),
        ],
        where=where,
        far=(4, 5, 8),
        vmem=24,
    )
    mlp_arrived = send(mlp_handed, OTHER_CORE)
    qkv_handed, qkv_kept, rim = call(
        attention_backward_kernel,
        [queries, keys, values, grad_context, row_segs, column_segs, log_total]
        + [cosine_table, signed_sine, first_normed],
        [((key_span, 3 * WIDTH + 384), BF), ((key_span, 384), BF)] + [((HALF, 2 * WIDTH), BF)],
        scratch=[(wide, F32), (wide, F32)],
        where=where,
    )
    qkv_arrived = send(qkv_handed, OTHER_CORE)
    rim_arrived = lax.ppermute(
        rim, "shard", [(i, i + 1) for i in range(1, 15, 2)] + [(i + 1, i) for i in range(1, 15, 2)]
    )
    stage = call(
        mlp_term_kernel,
        [mlp_handed, mlp_kept, mlp_arrived],
        [((2, 144, WIDTH), BF)] * 4 + [((8, 32, WIDTH), BF)] * 4,
        scratch=[((8, 144, WIDTH), BF), ((8, 128, WIDTH), BF)],
        where=where,
        after=[qkv_handed],
        flops=40_000_000_000,
    )
    z_parts, y_parts = stage[:4], stage[4:]
    x_parts = call(
        qkv_term_kernel,
        [qkv_handed, qkv_kept, qkv_arrived],
        [((4, 144, WIDTH), BF)] * 2,
        scratch=[((8, 144, WIDTH), BF)],
        where=where,
        after=[z_parts[0], rim_arrived],
        flops=40_000_000_000,
    )
    x_arrived = send(x_parts[1], ACROSS_X)
    z_arrived = [send(z_parts[step], Z_STEP[step]) for step in (1, 3)]
    z_arrived.append(send(hold(z_parts[2], z_arrived[0]), Z_STEP[2]))
    y_arrived = [send(y_parts[step], Y_STEP[step]) for step in (1, 3)]
    y_arrived.append(send(hold(y_parts[2], y_arrived[0]), Y_STEP[2]))
    (grad_tokens,) = call(
        token_grad_kernel,
        [tokens, qkv_handed, qkv_arrived, rim_arrived, wqkv_all, gain_table, grad_hidden],
        [(square, BF)],
        where=where,
        after=[x_parts[0]],
        flops=40_000_000_000,
    )
    own_across, sent_across = call(
        second_across_kernel,
        [z_parts[0], *z_arrived, y_parts[0], *y_arrived],
        [((272, WIDTH), BF)] * 2,
        where=where,
        after=[grad_tokens],
    )
    stage = call(
        second_along_kernel,
        [x_parts[0], x_arrived],
        [((144, WIDTH), BF)] * 4,
        where=where,
        after=[sent_across],
    )
    x_arrived = send(sent_across, ACROSS_X)
    z_arrived = [send(stage[step], Z_STEP[step]) for step in STEPS]
    ends = call(
        third_along_kernel,
        [own_across, x_arrived],
        [((32, WIDTH), BF)] * 4,
        scratch=[((4, 32, WIDTH), F32)],
        where=where,
    )
    stage = call(
        third_kernel,
        [own_across, x_arrived, stage[0], *z_arrived],
        [((72, WIDTH), BF)] * 4,
        scratch=[((288, WIDTH), F32)],
        where=where,
        after=[ends[0]],
    )
    y_arrived = [send(stage[step], Y_STEP[step]) for step in STEPS]
    z_arrived = [send(ends[step], Z_STEP[step]) for step in STEPS]
    part = [((104, WIDTH), BF)]
    (total,) = call(fourth_kernel, [stage[0], *y_arrived, ends[0], *z_arrived], part)
    (total,) = call(twin_sum_kernel, [total, send(total, TWIN_X)], part)
    quarters = [total] + [send(total, Y_STEP[4 - step]) for step in STEPS]
    columns = (48, 3 * WIDTH)
    grad_w_qkv, gain1, grad_w_in, gain2, grad_w_out, grad_w_down = call(
        final_kernel,
        [*quarters, w_qkv, norm1_gain[None, :], w_in, norm2_gain[None, :]],
        [(columns, F32), ((1, 48), F32), (columns, F32), ((1, 48), F32)]
        + [((48, WIDTH), F32), ((72, WIDTH), F32)],
        scratch=[((288, WIDTH), F32), ((128, WIDTH), F32)],
        where=where,
    )
    return (
        output, grad_tokens, gain1[0], grad_w_qkv, grad_w_out, gain2[0], grad_w_in, grad_w_down
    )


def solution(mesh):
    return jax.shard_map(
        shards,
        mesh=mesh,
        in_specs=(
            P(("rep", "shard"), None),
            P("rep", None),
            P("shard"),
            P("shard", None),
            P("shard", None),
            P("shard"),
            P("shard", None),
            P("shard", None),
            P(("rep", "shard"), None),
        ),
        out_specs=(
            P(("rep", "shard"), None),
            P(("rep", "shard"), None),
            P("shard"),
            P("shard", None),
            P("shard", None),
            P("shard"),
            P("shard", None),
            P("shard", None),
        ),
        check_vma=False,
    )
```
